256 devices in a mesh: row: 64 (over z_hi, y, x, core), col: 4 (over z_lo).
Axes of the slice: x: 4, y: 4, z: 8 (z_hi: 2, z_lo: 4; z = z_hi * 4 + z_lo), core: 2. Of those that a mesh axis runs over, the one named last changes fastest.
Arguments:
- block_rows: int32 [64, 4, 64], P('row', 'col'), may hold values from -1 to 251, as said below
- block_cols: int32 [64, 4, 64], P('row', 'col'), may hold values from -1 to 255, as said below
- block_values: bfloat16 [64, 4, 64, 256, 256], P('row', 'col'), may hold values from 0.0009994507 to 1
- near_values: bfloat16 [65536, 1024], P(('row', 'col')), may hold values from 0.0009994507 to 1
- hole_ids: int32 [65536], P(('row', 'col')), may hold values from 0 to 199
- start_codes: float32 [200, 64], replicated, may hold values from -6 to 6
Outputs:
- basis: float32 [65536, 64], P(('row', 'col'))
The draws below stay inside these ranges and needn't reach their ends.
Inputs may be any that keep to these rules, and one draw needn't show every extreme that they name: `block_rows`: A live slot of the device at band r and column index c names a block row of band r and a block column j * 4 + c * 4 / 4 + i with j > r and 0 <= i < 4 / 4. The device at band r has exactly (64 * (64 - 1 - r) + 64 - 2) // (64 - 1) live slots, placed first; the others hold -1 in both lists and their values are ignored. A block may be named by several slots; the affinity is then the sum. `block_cols`: see block_rows; empty slots hold -1 in the same places.
All inputs are finite; a program needn't handle non-finite values.
Results may differ from the reference program's by a relative error of at most 0.0063.
Values may be sent and summed in bfloat16 or wider, within the bound.
A program may use at most 128 MiB of HBM per device.

```python
import math
import jax
import jax.numpy as jnp
from jax import lax

BLK = 256
K = 64
HOLES = 200
ITERS = 3
RBD = 4
SLOTS = 64
BLOCKS = 256
ROWS = 65536
BAND = 1024
N_ROW = 64
N_COL = 4


def slot_pattern(key):
    key_rows, key_band, key_inner = jax.random.split(key, 3)
    quarter_blocks = RBD // N_COL
    shape_all = (N_ROW, N_COL, SLOTS)
    band_index = jnp.arange(N_ROW, dtype=jnp.int32)[:, None, None]
    col_index = jnp.arange(N_COL, dtype=jnp.int32)[None, :, None]
    slot_index = jnp.arange(SLOTS, dtype=jnp.int32)[None, None, :]
    first_slot = slot_index == 0
    ahead_bands = N_ROW - 1 - band_index
    row_offset = jnp.where(first_slot, RBD - 1, jax.random.randint(key_rows, shape_all, 0, RBD, dtype=jnp.int32))
    row_pick = band_index * RBD + row_offset
    later_band = band_index + 1 + jax.random.randint(key_band, shape_all, 0, N_ROW * 97, dtype=jnp.int32) % jnp.maximum(ahead_bands, 1)
    inner_pick = jnp.where(first_slot, quarter_blocks - 1, jax.random.randint(key_inner, shape_all, 0, quarter_blocks, dtype=jnp.int32))
    col_pick = later_band * RBD + col_index * quarter_blocks + inner_pick
    live_count = (SLOTS * ahead_bands + N_ROW - 2) // (N_ROW - 1)
    live_slot = slot_index < live_count
    return (jnp.where(live_slot, row_pick, -1).astype(jnp.int32), jnp.where(live_slot, col_pick, -1).astype(jnp.int32))


def draw_block_rows(key, part):
    return slot_pattern(key)[0]


def draw_block_cols(key, part):
    return slot_pattern(key)[1]


def touch_ends(result, key, smallest, largest):
    extent = result.shape
    spot = [jax.random.randint(jax.random.fold_in(key, axis), (), 0, extent[axis]) for axis in range(len(extent))]
    result = result.at[tuple(spot)].set(smallest)
    longest = extent.index(max(extent))
    spot[longest] = (spot[longest] + 1) % extent[longest]
    return result.at[tuple(spot)].set(largest)


def levels(own_key, extent, shards, least, top_value):
    gain = 1.0
    for axis_at, blocks in shards:
        steps = jax.random.uniform(jax.random.fold_in(jax.random.fold_in(own_key, 6), axis_at), (blocks,), jnp.float32, least / len(shards), top_value / len(shards))
        gain = gain * jnp.repeat(jnp.exp(steps), extent[axis_at] // blocks).reshape((-1,) + (1,) * (len(extent) - 1 - axis_at))
    return gain


def gaussian(rng, shape, scale, most, held_as=jnp.bfloat16):
    return jnp.clip(scale * jax.random.normal(rng, shape, jnp.float32), -most, most).astype(held_as)


def setup_inputs(seed: int = 0) -> dict:
    streams_of = jax.random.split(jax.random.key(seed), 7)
    block_rows = draw_block_rows(jax.random.fold_in(streams_of[6], 71), 0)
    block_cols = draw_block_cols(jax.random.fold_in(streams_of[6], 71), 0)
    block_values = jnp.clip(jnp.exp(math.log(1.0) - 6.9083047 * jax.random.uniform(streams_of[2], (N_ROW, N_COL, SLOTS, BLK, BLK), jnp.float32) ** levels(streams_of[2], (N_ROW, N_COL, SLOTS, BLK, BLK), ((0, 64), (1, 4)), -0.2, 0.2)), 0.0009994507, 1.0).astype(jnp.bfloat16)
    near_values = jnp.clip(jnp.exp(math.log(1.0) - 6.9083047 * jax.random.uniform(streams_of[3], (ROWS, BAND), jnp.float32) ** levels(streams_of[3], (ROWS, BAND), ((0, 256),), -0.2, 0.2)), 0.0009994507, 1.0).astype(jnp.bfloat16)
    hole_ids = touch_ends(jax.random.randint(streams_of[4], (ROWS,), 0, HOLES), jax.random.fold_in(streams_of[4], 1), 0, HOLES - 1).astype(jnp.int32)
    start_codes = gaussian(streams_of[5], (HOLES, K), 1.0, 6.0, jnp.float32)
    return dict(block_rows=block_rows, block_cols=block_cols, block_values=block_values, near_values=near_values, hole_ids=hole_ids, start_codes=start_codes)


def apply_affinity(probe, block_rows, block_cols, block_values, near_values):
    col_width = probe.shape[1]
    tiles = probe.reshape(BLOCKS, BLK, col_width)
    slot_rows = block_rows.reshape(N_ROW * N_COL, SLOTS)
    slot_cols = block_cols.reshape(N_ROW * N_COL, SLOTS)
    slot_vals = block_values.reshape(N_ROW * N_COL, SLOTS, BLK, BLK)

    def sweep_device(running, slot_data):
        row_ids, col_ids, vals = slot_data
        live_slot = row_ids >= 0
        safe_rows = jnp.where(live_slot, row_ids, 0).astype(jnp.int32)
        safe_cols = jnp.where(live_slot, col_ids, 0).astype(jnp.int32)
        vals_wide = vals.astype(jnp.float32)
        weight_live = live_slot.astype(jnp.float32)[:, None, None]
        forward = jnp.einsum('sij,sjk->sik', vals_wide, tiles[safe_cols].astype(jnp.float32)) * weight_live
        backward = jnp.einsum('sji,sjk->sik', vals_wide, tiles[safe_rows].astype(jnp.float32)) * weight_live
        running = running.at[safe_rows].add(forward)
        running = running.at[safe_cols].add(backward)
        return (running, None)
    running = lax.scan(sweep_device, jnp.zeros((BLOCKS, BLK, col_width), jnp.float32), (slot_rows, slot_cols, slot_vals))[0]
    near_wide = near_values.reshape(N_ROW, BAND, BAND).astype(jnp.float32)
    band_probe = probe.reshape(N_ROW, BAND, col_width).astype(jnp.float32)
    near_part = jnp.einsum('bij,bjk->bik', near_wide, band_probe) + jnp.einsum('bji,bjk->bik', near_wide, band_probe)
    return running.reshape(ROWS, col_width) + near_part.reshape(ROWS, col_width)

def reference(block_rows, block_cols, block_values, near_values, hole_ids, start_codes):
    degree = apply_affinity(jnp.ones((ROWS, 1), jnp.bfloat16), block_rows, block_cols, block_values, near_values)[:, 0]
    scale_root = 1.0 / jnp.sqrt(degree)
    basis_now = start_codes[hole_ids]
    for sweep_index in range(ITERS):
        probe = (scale_root[:, None] * basis_now).astype(jnp.bfloat16)
        image = scale_root[:, None] * apply_affinity(probe, block_rows, block_cols, block_values, near_values)
        gram_matrix = jnp.dot(image.T, image, precision=lax.Precision.HIGHEST) / ROWS
        factor = jnp.linalg.cholesky(gram_matrix)
        basis_now = lax.linalg.triangular_solve(factor, image, left_side=False, lower=True, transpose_a=True)
    return basis_now
```

```python
import jax
import jax.numpy as jnp
from jax import lax
from jax.experimental import pallas as pl
from jax.experimental.pallas import tpu as pltpu
from jax.sharding import PartitionSpec as P

ITERS = 3
MESH = pl.DeviceIdType.MESH
F32 = jnp.float32
BF16 = jnp.bfloat16
HIGH = lax.Precision.HIGHEST

SLOTS = 64
BLK = 256
K = 64
BANDS = 64
CHIPS = 32
PLANE = 16
COLS = 4

ROW, COL, PREV_COL, PREV_ROW, LAST_COL, LAST_ROW = (i * SLOTS for i in range(6))


def remote(src, dst, send_sem, recv_sem, device):
    return pltpu.make_async_remote_copy(
        src_ref=src,
        dst_ref=dst,
        send_sem=send_sem,
        recv_sem=recv_sem,
        device_id=device,
        device_id_type=MESH,
    )


def nt(a, b, precision=None):
    return lax.dot_general(
        a, b, (((1,), (1,)), ((), ())), preferred_element_type=F32, precision=precision
    )


def nn(a, b, precision=None):
    return lax.dot_general(
        a, b, (((1,), (0,)), ((), ())), preferred_element_type=F32, precision=precision
    )


def loop(first, last, body):
    def step(i, carry):
        body(i)
        return carry

    lax.fori_loop(first, last, step, 0)


def inverse_factor(gram):
    row = lax.broadcasted_iota(jnp.int32, (K, 2 * K), 0)
    lane = lax.broadcasted_iota(jnp.int32, (K, 2 * K), 1)
    wide = jnp.concatenate([gram, jnp.zeros((K, K), F32)], axis=1)
    wide = wide + jnp.where(lane == row + K, 1.0, 0.0).astype(F32)
    tiles = [wide[8 * t : 8 * t + 8, :] for t in range(K // 8)]
    sub = lax.broadcasted_iota(jnp.int32, (8, 1), 0)
    for j in range(K - 1):
        t, s = divmod(j, 8)
        pivot = tiles[t][s : s + 1, :]
        scaled = pivot / pivot[:, j : j + 1]
        for u in range(t, K // 8):
            factor = tiles[u][:, j : j + 1]
            if u == t:
                if s == 7:
                    continue
                factor = jnp.where(sub > s, factor, 0.0)
            tiles[u] = tiles[u] - factor * scaled
    done = jnp.concatenate(tiles, axis=0)
    diag = jnp.sum(jnp.where(lane == row, done, 0.0), axis=1, keepdims=True)
    return done[:, K:] / jnp.sqrt(diag)


def kernel(
    idx,
    vals_hbm,
    near_hbm,
    holes,
    codes,
    out,
    vals,
    near,
    gath,
    band,
    chain_c,
    chain_f,
    deg_c,
    deg_f,
    t1,
    r1,
    t2,
    r2,
    xs,
    xr,
    wq,
    rq,
    dt1,
    dr1,
    dt2,
    dr2,
    dxs,
    dxr,
    dwq,
    drq,
    acc,
    dacc,
    basis,
    gram_send,
    gram_core,
    gram_plane,
    gram_z,
    gram_back,
    load_sem,
    g_s,
    g_r,
    c_s,
    c_r,
    x_s,
    x_r,
    f_s,
    f_r,
    b_s,
    b_r,
    t1_s,
    t1_r,
    t2_s,
    t2_r,
    z_s,
    z_r,
    q_s,
    q_r,
    a1_s,
    a1_r,
    a2_s,
    a2_r,
    a3_s,
    a3_r,
    a4_s,
    a4_r,
):
    r = lax.axis_index("row")
    c = lax.axis_index("col")
    k = r % 2
    chip = r // 2
    p = chip % PLANE
    zh = r // 32
    z = zh * COLS + c
    sib = (r + 1 - 2 * k, c)
    far = ((1 - zh) * 32 + p * 2 + k, c)

    def plane(i):
        return (zh * 32 + i * 2 + k, c)

    def in_band(i):
        return (r, i)

    def along_z(i):
        return ((i // COLS) * 32 + p * 2 + k, i % COLS)

    parts = 4
    part = SLOTS // parts
    near_load = pltpu.make_async_copy(near_hbm, near, load_sem.at[parts])
    near_load.start()
    loads = [
        pltpu.make_async_copy(
            vals_hbm.at[pl.ds(i * part, part)], vals.at[pl.ds(i * part, part)], load_sem.at[i]
        )
        for i in range(parts)
    ]
    for load in loads:
        load.start()

    barrier = pltpu.get_barrier_semaphore()
    pl.semaphore_signal(barrier, inc=1, device_id=sib, device_id_type=MESH)
    for d in range(1, PLANE):
        pl.semaphore_signal(
            barrier, inc=1, device_id=plane((p + d) % PLANE), device_id_type=MESH
        )
    for d in range(1, 2 * COLS):
        pl.semaphore_signal(
            barrier, inc=1, device_id=along_z((z + d) % (2 * COLS)), device_id_type=MESH
        )

    chain_c[0] = jnp.zeros((K, BLK), F32)
    chain_f[0] = jnp.zeros((K, BLK), F32)
    deg_c[0] = jnp.zeros((1, BLK), F32)
    deg_f[0] = jnp.zeros((1, BLK), F32)

    def mirror_send(m, chain, t1, r1, t2, r2):
        kind = t1.dtype

        def to_core(i):
            at = CHIPS - 1 - i
            t1[at] = chain[idx[LAST_COL + at * 2 + 1 - k]].astype(kind)
            remote(t1.at[at], r1.at[at], t1_s.at[m, at], t1_r.at[m, at], sib).start()

        loop(0, CHIPS - chip - k, to_core)

        def to_chip(i):
            at = CHIPS - 1 - i
            to, half = at % PLANE, at // PLANE
            remote(t1.at[at], r1.at[at], t1_s.at[m, at], t1_r.at[m, at], sib).wait_recv()
            both = (chain[idx[LAST_COL + at * 2 + k]] + r1[at].astype(F32)).astype(kind)

            @pl.when(to == p)
            def _():
                r2[PLANE + p] = both

            @pl.when(to != p)
            def _():
                t2[at] = both
                remote(
                    t2.at[at],
                    r2.at[half * PLANE + p],
                    t2_s.at[m, at],
                    t2_r.at[m, half * PLANE + p],
                    plane(to),
                ).start()

        loop(0, CHIPS - 1 - chip, to_chip)

    def mirror_cross(m, r2, t2, xs, xr):
        @pl.when(zh == 0)
        def _():
            def add(i, total):
                source = (p + i) % PLANE
                at = PLANE + source
                remote(t2.at[at], r2.at[at], t2_s.at[m, at], t2_r.at[m, at], plane(source)).wait_recv()
                return total + r2[at].astype(F32)

            xs[...] = lax.fori_loop(1, PLANE, add, r2[PLANE + p].astype(F32))
            remote(xs, xr, z_s.at[m], z_r.at[m], far).start()

    def mirror_sum(m, acc, t1, r1, t2, r2, xs, xr):
        def add(i, total):
            at = zh * PLANE + i
            remote(t2.at[at], r2.at[at], t2_s.at[m, at], t2_r.at[m, at], plane(i)).wait_recv()
            return total + r2[at].astype(F32)

        acc[...] += lax.fori_loop(0, p, add, jnp.zeros(acc.shape, F32))

        @pl.when(k == 1)
        def _():
            remote(
                t1.at[chip], r1.at[chip], t1_s.at[m, chip], t1_r.at[m, chip], sib
            ).wait_recv()
            acc[...] += r1[chip].astype(F32)

        @pl.when(zh == 1)
        def _():
            remote(xs, xr, z_s.at[m], z_r.at[m], far).wait_recv()
            acc[...] += xr[...]

    def mirror_done(m, t1, r1, t2, r2, xs, xr):
        def core_sent(i):
            at = CHIPS - 1 - i
            remote(t1.at[at], r1.at[at], t1_s.at[m, at], t1_r.at[m, at], sib).wait_send()

        loop(0, CHIPS - chip - k, core_sent)

        def chip_sent(i):
            at = CHIPS - 1 - i

            @pl.when(at % PLANE != p)
            def _():
                remote(
                    t2.at[at], r2.at[at], t2_s.at[m, at], t2_r.at[m, at], plane(at % PLANE)
                ).wait_send()

        loop(0, CHIPS - 1 - chip, chip_sent)

        @pl.when(zh == 0)
        def _():
            remote(xs, xr, z_s.at[m], z_r.at[m], far).wait_send()

    def band_send(m, wq, rq):
        for d in range(1, COLS):
            to = (c + d) % COLS
            remote(wq.at[to], rq.at[c], q_s.at[m, to], q_r.at[m, c], in_band(to)).start()

    def band_sum(m, acc, wq, rq):
        for d in range(1, COLS):
            at = (c + d) % COLS
            remote(wq.at[at], rq.at[at], q_s.at[m, at], q_r.at[m, at], in_band(at)).wait_recv()
            acc[...] += rq[at].astype(F32)

    def band_done(m, wq, rq):
        for d in range(1, COLS):
            at = (c + d) % COLS
            remote(wq.at[at], rq.at[at], q_s.at[m, at], q_r.at[m, at], in_band(at)).wait_send()

    ones = jnp.ones((8, BLK), BF16)
    for i in range(parts):
        loads[i].wait()

        def sums(s):
            deg_c[s + 1] = deg_c[idx[PREV_COL + s]] + nn(ones, vals[s])[0:1]
            deg_f[s + 1] = deg_f[idx[PREV_ROW + s]] + nt(ones, vals[s])[0:1]

        loop(i * part, (i + 1) * part, sums)
    near_load.wait()
    pl.semaphore_wait(barrier, 1 + PLANE - 1 + 2 * COLS - 1)

    mirror_send(0, deg_c, dt1, dr1, dt2, dr2)
    own_sum = jnp.zeros((1, BLK), F32)
    for q in range(COLS):
        tile = near[:, q * BLK : (q + 1) * BLK]
        own_sum = own_sum + nt(ones, tile)[0:1]
        dwq[q] = deg_f[idx[LAST_ROW + q]] + nn(ones, tile)[0:1]
    dacc[...] = own_sum + dwq[c]
    band_send(0, dwq, drq)

    hole = holes[...]
    onehot = jnp.where(
        lax.broadcasted_iota(jnp.int32, (codes.shape[0], BLK), 0) == hole, 1.0, 0.0
    ).astype(F32)
    basis[...] = lax.dot_general(
        codes[...], onehot, (((0,), (0,)), ((), ())), preferred_element_type=F32, precision=HIGH
    )

    mirror_cross(0, dr2, dt2, dxs, dxr)
    band_sum(0, dacc, dwq, drq)
    mirror_sum(0, dacc, dt1, dr1, dt2, dr2, dxs, dxr)
    mirror_done(0, dt1, dr1, dt2, dr2, dxs, dxr)
    band_done(0, dwq, drq)
    scale = 1.0 / jnp.sqrt(dacc[...])

    def gather_copy(send, recv, at, device):
        return remote(gath.at[at], gath.at[at], send, recv, device)

    def sweep(it):
        probe = (scale * basis[...]).astype(BF16)
        gath[r] = probe
        band[c] = probe

        for d in range(1, COLS):
            to = (c + d) % COLS
            remote(band.at[c], band.at[c], b_s.at[to], b_r.at[c], in_band(to)).start()

        @pl.when(zh == 1)
        def _():
            gather_copy(x_s.at[0], x_r.at[0], r, far).start()

        loop(0, p, lambda i: gather_copy(g_s.at[i], g_r.at[p], r, plane(i)).start())

        @pl.when(k == 1)
        def _():
            gather_copy(f_s.at[r], f_r.at[r], r, sib).start()

        for d in range(1, COLS):
            at = (c + d) % COLS
            remote(band.at[at], band.at[at], b_s.at[at], b_r.at[at], in_band(at)).wait_recv()

        cross = 32 + p * 2 + k

        @pl.when(zh == 0)
        def _():
            gather_copy(x_s.at[0], x_r.at[0], cross, far).wait_recv()

            def to_plane(i):
                to = (p + i) % PLANE
                gather_copy(c_s.at[to], c_r.at[p], cross, plane(to)).start()

            loop(1, PLANE, to_plane)
            gather_copy(f_s.at[cross], f_r.at[cross], cross, sib).start()

        def backward(s):
            chain_c[s + 1] = chain_c[idx[PREV_COL + s]] + nn(band[idx[ROW + s]], vals[s])

        loop(0, SLOTS, backward)
        mirror_send(1, chain_c, t1, r1, t2, r2)

        def own_pass(i):
            at = zh * 32 + i * 2 + k
            gather_copy(g_s.at[i], g_r.at[i], at, plane(i)).wait_recv()
            gather_copy(f_s.at[at], f_r.at[at], at, sib).start()

        loop(p + 1, PLANE, own_pass)

        own = jnp.zeros((K, BLK), F32)
        for q in range(COLS):
            own = own + nt(band[q], near[:, q * BLK : (q + 1) * BLK])
        acc[...] = own

        @pl.when(zh == 0)
        def _():
            def cross_pass(i):
                source = (p + i) % PLANE
                at = 32 + source * 2 + k
                gather_copy(c_s.at[source], c_r.at[source], at, plane(source)).wait_recv()
                gather_copy(f_s.at[at], f_r.at[at], at, sib).start()

            loop(1, PLANE, cross_pass)

            def cross_core(i):
                at = 32 + i * 2 + 1 - k
                gather_copy(f_s.at[at], f_r.at[at], at, sib).wait_recv()

            loop(0, PLANE, cross_core)

        def own_core(i):
            at = zh * 32 + i * 2 + 1 - k
            gather_copy(f_s.at[at], f_r.at[at], at, sib).wait_recv()

        loop(p + k, PLANE, own_core)

        def forward(s):
            chain_f[s + 1] = chain_f[idx[PREV_ROW + s]] + nt(gath[idx[COL + s]], vals[s])

        loop(0, SLOTS, forward)
        for q in range(COLS):
            total = chain_f[idx[LAST_ROW + q]] + nn(probe, near[:, q * BLK : (q + 1) * BLK])
            wq[q] = total.astype(BF16)

            @pl.when(c == q)
            def _():
                acc[...] += total

        band_send(1, wq, rq)

        @pl.when(zh == 0)
        def _():
            def plane_sent(i):
                to = (p + i) % PLANE
                gather_copy(c_s.at[to], c_r.at[p], cross, plane(to)).wait_send()

            loop(1, PLANE, plane_sent)

            def cross_sent(i):
                at = 32 + i * 2 + k
                gather_copy(f_s.at[at], f_r.at[at], at, sib).wait_send()

            loop(0, PLANE, cross_sent)

        def own_sent(i):
            at = zh * 32 + i * 2 + k
            gather_copy(f_s.at[at], f_r.at[at], at, sib).wait_send()

        loop(p + 1, PLANE, own_sent)

        mirror_cross(1, r2, t2, xs, xr)
        band_sum(1, acc, wq, rq)
        mirror_sum(1, acc, t1, r1, t2, r2, xs, xr)

        image = scale * acc[...]
        gram = nt(image, image, HIGH)

        low = jnp.concatenate([gram[0:16], gram[16:32]], axis=1)
        high = jnp.concatenate([gram[32:48], gram[48:64]], axis=1)
        gram_send[it] = jnp.where(k == 0, high, low)
        core = remote(gram_send.at[it], gram_core.at[it], a1_s.at[it], a1_r.at[it], sib)
        core.start()
        core.wait_recv()
        gram_plane[it, p] = jnp.where(k == 0, low, high) + gram_core[it]

        def plane_copy(to, source):
            return remote(
                gram_plane.at[it, source],
                gram_plane.at[it, source],
                a2_s.at[it, to],
                a2_r.at[it, source],
                plane(to if source is p else source),
            )

        def plane_start(i):
            to = (p + i) % PLANE
            plane_copy(to, p).start()

        loop(1, PLANE, plane_start)

        def plane_wait(i):
            source = (p + i) % PLANE
            plane_copy(source, source).wait_recv()

        loop(1, PLANE, plane_wait)
        total = gram_plane[it, 0]
        for i in range(1, PLANE):
            total = total + gram_plane[it, i]
        gram_z[it, z] = total
        for d in range(1, 2 * COLS):
            to = (z + d) % (2 * COLS)
            remote(
                gram_z.at[it, z], gram_z.at[it, z], a3_s.at[it, to], a3_r.at[it, z], along_z(to)
            ).start()
        for d in range(1, 2 * COLS):
            at = (z + d) % (2 * COLS)
            remote(
                gram_z.at[it, at], gram_z.at[it, at], a3_s.at[it, at], a3_r.at[it, at], along_z(at)
            ).wait_recv()
        total = gram_z[it, 0]
        for i in range(1, 2 * COLS):
            total = total + gram_z[it, i]
        gram_back[it, k] = total
        back = remote(
            gram_back.at[it, k], gram_back.at[it, k], a4_s.at[it], a4_r.at[it, k], sib
        )
        back.start()
        remote(
            gram_back.at[it, 1 - k], gram_back.at[it, 1 - k], a4_s.at[it], a4_r.at[it, 1 - k], sib
        ).wait_recv()
        low = gram_back[it, 0]
        high = gram_back[it, 1]
        gram = jnp.concatenate([low[:, :K], low[:, K:], high[:, :K], high[:, K:]], axis=0)
        total_rows = BLK * BANDS * COLS
        basis[...] = nn(inverse_factor(gram * (1.0 / total_rows)), image, HIGH)

        for d in range(1, COLS):
            to = (c + d) % COLS
            remote(band.at[c], band.at[c], b_s.at[to], b_r.at[c], in_band(to)).wait_send()

        @pl.when(zh == 1)
        def _():
            gather_copy(x_s.at[0], x_r.at[0], r, far).wait_send()

        loop(0, p, lambda i: gather_copy(g_s.at[i], g_r.at[p], r, plane(i)).wait_send())

        @pl.when(k == 1)
        def _():
            gather_copy(f_s.at[r], f_r.at[r], r, sib).wait_send()

        mirror_done(1, t1, r1, t2, r2, xs, xr)
        band_done(1, wq, rq)
        core.wait_send()

        def plane_done(i):
            to = (p + i) % PLANE
            plane_copy(to, p).wait_send()

        loop(1, PLANE, plane_done)
        for d in range(1, 2 * COLS):
            to = (z + d) % (2 * COLS)
            remote(
                gram_z.at[it, z], gram_z.at[it, z], a3_s.at[it, to], a3_r.at[it, z], along_z(to)
            ).wait_send()
        back.wait_send()

    loop(0, ITERS, sweep)
    out[...] = basis[...].T


def shards(block_rows, block_cols, block_values, near_values, hole_ids, start_codes):
    row_index = lax.axis_index("row")
    rows = block_rows.reshape(SLOTS)
    cols = block_cols.reshape(SLOTS)
    live = rows >= 0
    local_row = jnp.where(live, rows - row_index * COLS, -1)
    local_col = jnp.where(live, cols // COLS, -1)
    slot = jnp.arange(SLOTS, dtype=jnp.int32)

    def previous(keys):
        same = (keys[None, :] == keys[:, None]) & (slot[None, :] < slot[:, None])
        return jnp.max(jnp.where(same, slot[None, :] + 1, 0), axis=1)

    def last(keys):
        same = keys[None, :] == slot[:, None]
        return jnp.max(jnp.where(same, slot[None, :] + 1, 0), axis=1)

    idx = jnp.concatenate(
        [
            jnp.maximum(local_row, 0),
            jnp.maximum(local_col, 0),
            previous(local_col),
            previous(local_row),
            last(local_col),
            last(local_row),
        ]
    ).astype(jnp.int32)
    block = (K, BLK)
    line = (1, BLK)
    dma = pltpu.SemaphoreType.DMA
    return pl.pallas_call(
        kernel,
        name="subspace",
        out_shape=jax.ShapeDtypeStruct((BLK, K), F32),
        in_specs=[
            pl.BlockSpec(memory_space=pltpu.SMEM),
            pl.BlockSpec(memory_space=pl.ANY),
            pl.BlockSpec(memory_space=pl.ANY),
            pl.BlockSpec(memory_space=pltpu.VMEM),
            pl.BlockSpec(memory_space=pltpu.VMEM),
        ],
        out_specs=pl.BlockSpec(memory_space=pltpu.VMEM),
        scratch_shapes=[
            pltpu.VMEM((SLOTS, BLK, BLK), BF16),
            pltpu.VMEM((BLK, COLS * BLK), BF16),
            pltpu.VMEM((BANDS, *block), BF16),
            pltpu.VMEM((COLS, *block), BF16),
            pltpu.VMEM((SLOTS + 1, *block), F32),
            pltpu.VMEM((SLOTS + 1, *block), F32),
            pltpu.VMEM((SLOTS + 1, *line), F32),
            pltpu.VMEM((SLOTS + 1, *line), F32),
            pltpu.VMEM((CHIPS, *block), BF16),
            pltpu.VMEM((CHIPS, *block), BF16),
            pltpu.VMEM((CHIPS, *block), BF16),
            pltpu.VMEM((CHIPS, *block), BF16),
            pltpu.VMEM(block, F32),
            pltpu.VMEM(block, F32),
            pltpu.VMEM((COLS, *block), BF16),
            pltpu.VMEM((COLS, *block), BF16),
            pltpu.VMEM((CHIPS, *line), F32),
            pltpu.VMEM((CHIPS, *line), F32),
            pltpu.VMEM((CHIPS, *line), F32),
            pltpu.VMEM((CHIPS, *line), F32),
            pltpu.VMEM(line, F32),
            pltpu.VMEM(line, F32),
            pltpu.VMEM((COLS, *line), F32),
            pltpu.VMEM((COLS, *line), F32),
            pltpu.VMEM(block, F32),
            pltpu.VMEM(line, F32),
            pltpu.VMEM(block, F32),
            pltpu.VMEM((ITERS, 16, 2 * K), F32),
            pltpu.VMEM((ITERS, 16, 2 * K), F32),
            pltpu.VMEM((ITERS, PLANE, 16, 2 * K), F32),
            pltpu.VMEM((ITERS, 2 * COLS, 16, 2 * K), F32),
            pltpu.VMEM((ITERS, 2, 16, 2 * K), F32),
            dma((5,)),
            dma((PLANE,)),
            dma((PLANE,)),
            dma((PLANE,)),
            dma((PLANE,)),
            dma((1,)),
            dma((1,)),
            dma((BANDS,)),
            dma((BANDS,)),
            dma((COLS,)),
            dma((COLS,)),
            dma((2, CHIPS)),
            dma((2, CHIPS)),
            dma((2, CHIPS)),
            dma((2, CHIPS)),
            dma((2,)),
            dma((2,)),
            dma((2, COLS)),
            dma((2, COLS)),
            dma((ITERS,)),
            dma((ITERS,)),
            dma((ITERS, PLANE)),
            dma((ITERS, PLANE)),
            dma((ITERS, 2 * COLS)),
            dma((ITERS, 2 * COLS)),
            dma((ITERS,)),
            dma((ITERS, 2)),
        ],
        compiler_params=pltpu.CompilerParams(
            collective_id=0, has_side_effects=True, vmem_limit_bytes=56 << 20
        ),
    )(
        idx,
        block_values.reshape(SLOTS, BLK, BLK),
        near_values,
        hole_ids.reshape(1, BLK),
        start_codes,
    )


def solution(mesh):
    return jax.shard_map(
        shards,
        mesh=mesh,
        in_specs=(
            P("row", "col", None),
            P("row", "col", None),
            P("row", "col", None, None, None),
            P(("row", "col"), None),
            P(("row", "col")),
            P(),
        ),
        out_specs=P(("row", "col"), None),
        check_vma=False,
    )
```

```python
import jax
import jax.numpy as jnp
from jax import lax
from jax.experimental import pallas as pl
from jax.experimental.pallas import tpu as pltpu
from jax.sharding import PartitionSpec as P

ITERS = 3
MESH = pl.DeviceIdType.MESH
F32 = jnp.float32
BF16 = jnp.bfloat16
HIGH = lax.Precision.HIGHEST

SLOTS = 64
BLK = 256
K = 64
BANDS = 64
CHIPS = 32
PLANE = 16
COLS = 4
SIDE = 4
HALF = K // 2
GROUP = 32
SUMS = 16

ROW, COL, PREV_COL, PREV_ROW, LAST_COL, LAST_ROW = (i * SLOTS for i in range(6))


def remote(src, dst, send_sem, recv_sem, device):
    return pltpu.make_async_remote_copy(
        src_ref=src,
        dst_ref=dst,
        send_sem=send_sem,
        recv_sem=recv_sem,
        device_id=device,
        device_id_type=MESH,
    )


def nt(a, b, precision=None):
    return lax.dot_general(
        a, b, (((1,), (1,)), ((), ())), preferred_element_type=F32, precision=precision
    )


def nn(a, b, precision=None):
    return lax.dot_general(
        a, b, (((1,), (0,)), ((), ())), preferred_element_type=F32, precision=precision
    )


def loop(first, last, body):
    def step(i, carry):
        body(i)
        return carry

    lax.fori_loop(first, last, step, 0)


def inverse_factor(gram):
    row = lax.broadcasted_iota(jnp.int32, (K, 2 * K), 0)
    lane = lax.broadcasted_iota(jnp.int32, (K, 2 * K), 1)
    wide = jnp.concatenate([gram, jnp.zeros((K, K), F32)], axis=1)
    wide = wide + jnp.where(lane == row + K, 1.0, 0.0).astype(F32)
    tiles = [wide[8 * t : 8 * t + 8, :] for t in range(K // 8)]
    sub = lax.broadcasted_iota(jnp.int32, (8, 1), 0)
    for j in range(K - 1):
        t, s = divmod(j, 8)
        pivot = tiles[t][s : s + 1, :]
        scaled = pivot / pivot[:, j : j + 1]
        for u in range(t, K // 8):
            factor = tiles[u][:, j : j + 1]
            if u == t:
                if s == 7:
                    continue
                factor = jnp.where(sub > s, factor, 0.0)
            tiles[u] = tiles[u] - factor * scaled
    done = jnp.concatenate(tiles, axis=0)
    diag = jnp.sum(jnp.where(lane == row, done, 0.0), axis=1, keepdims=True)
    return done[:, K:] / jnp.sqrt(diag)


def kernel(
    idx,
    vals_hbm,
    near_hbm,
    holes,
    codes,
    out,
    vals,
    near,
    raw,
    band_raw,
    cross_lines,
    band_lines,
    gath,
    band,
    chain_c,
    chain_f,
    deg_c,
    deg_f,
    t1,
    r1,
    t2,
    r2,
    xs,
    xr,
    wq,
    rq,
    dt1,
    dr1,
    dt2,
    dr2,
    dxs,
    dxr,
    dwq,
    drq,
    acc,
    dacc,
    inverse,
    gram_send,
    gram_core,
    gram_plane,
    gram_z,
    gram_back,
    load_sem,
    g_s,
    g_r,
    c_s,
    c_r,
    x_s,
    x_r,
    c2_s,
    c2_r,
    f_s,
    f_r,
    b_s,
    b_r,
    lb_s,
    lb_r,
    lx_s,
    lx_r,
    lc_s,
    lc_r,
    t1_s,
    t1_r,
    t2_s,
    t2_r,
    z_s,
    z_r,
    q_s,
    q_r,
    a1_s,
    a1_r,
    a2_s,
    a2_r,
    a3_s,
    a3_r,
    a4_s,
    a4_r,
):
    r = lax.axis_index("row")
    c = lax.axis_index("col")
    k = r % 2
    chip = r // 2
    p = chip % PLANE
    y = p // SIDE
    x = p % SIDE
    zh = r // 32
    z = zh * COLS + c
    sib = (r + 1 - 2 * k, c)
    far = ((1 - zh) * 32 + p * 2 + k, c)

    def plane(i):
        return (zh * 32 + i * 2 + k, c)

    def in_band(i):
        return (r, i)

    def along_z(i):
        return ((i // COLS) * 32 + p * 2 + k, i % COLS)

    parts = 4
    part = SLOTS // parts
    near_load = pltpu.make_async_copy(near_hbm, near, load_sem.at[parts])
    near_load.start()
    loads = [
        pltpu.make_async_copy(
            vals_hbm.at[pl.ds(i * part, part)], vals.at[pl.ds(i * part, part)], load_sem.at[i]
        )
        for i in range(parts)
    ]
    for load in loads:
        load.start()

    barrier = pltpu.get_barrier_semaphore()
    pl.semaphore_signal(barrier, inc=1, device_id=sib, device_id_type=MESH)
    for d in range(1, PLANE):
        pl.semaphore_signal(
            barrier, inc=1, device_id=plane((p + d) % PLANE), device_id_type=MESH
        )
    for d in range(1, 2 * COLS):
        pl.semaphore_signal(
            barrier, inc=1, device_id=along_z((z + d) % (2 * COLS)), device_id_type=MESH
        )

    chain_c[0] = jnp.zeros((K, BLK), F32)
    chain_f[0] = jnp.zeros((K, BLK), F32)
    deg_c[0] = jnp.zeros((1, BLK), F32)
    deg_f[0] = jnp.zeros((1, BLK), F32)

    def each_later(body, first):
        @pl.when(zh == 0)
        def _():
            loop(1, PLANE + 1, lambda i: body(PLANE + (p + i) % PLANE))

        loop(first, PLANE, lambda i: body(zh * PLANE + i))

    def mirror_core(m, chain, t1, r1):
        kind = t1.dtype

        def to_core(at):
            t1[at] = chain[idx[LAST_COL + at * 2 + 1 - k]].astype(kind)
            remote(t1.at[at], r1.at[at], t1_s.at[m, at], t1_r.at[m, at], sib).start()

        each_later(to_core, p + k)

    def mirror_plane(m, chain, t1, r1, t2, r2):
        kind = t2.dtype

        def to_chip(at):
            to, half = at % PLANE, at // PLANE
            remote(t1.at[at], r1.at[at], t1_s.at[m, at], t1_r.at[m, at], sib).wait_recv()
            both = (chain[idx[LAST_COL + at * 2 + k]] + r1[at].astype(F32)).astype(kind)

            @pl.when(to == p)
            def _():
                r2[PLANE + p] = both

            @pl.when(to != p)
            def _():
                t2[at] = both
                remote(
                    t2.at[at],
                    r2.at[half * PLANE + p],
                    t2_s.at[m, at],
                    t2_r.at[m, half * PLANE + p],
                    plane(to),
                ).start()

        each_later(to_chip, p + 1)

    def mirror_cross(m, r2, t2, xs, xr):
        @pl.when(zh == 0)
        def _():
            def add(i, total):
                source = (p + i) % PLANE
                at = PLANE + source
                remote(t2.at[at], r2.at[at], t2_s.at[m, at], t2_r.at[m, at], plane(source)).wait_recv()
                return total + r2[at].astype(F32)

            xs[...] = lax.fori_loop(1, PLANE, add, r2[PLANE + p].astype(F32))
            remote(xs, xr, z_s.at[m], z_r.at[m], far).start()

    def mirror_sum(m, acc, t1, r1, t2, r2, xs, xr):
        def add(i, total):
            at = zh * PLANE + i
            remote(t2.at[at], r2.at[at], t2_s.at[m, at], t2_r.at[m, at], plane(i)).wait_recv()
            return total + r2[at].astype(F32)

        acc[...] += lax.fori_loop(0, p, add, jnp.zeros(acc.shape, F32))

        @pl.when(k == 1)
        def _():
            remote(
                t1.at[chip], r1.at[chip], t1_s.at[m, chip], t1_r.at[m, chip], sib
            ).wait_recv()
            acc[...] += r1[chip].astype(F32)

        @pl.when(zh == 1)
        def _():
            remote(xs, xr, z_s.at[m], z_r.at[m], far).wait_recv()
            acc[...] += xr[...]

    def mirror_done(m, t1, r1, t2, r2, xs, xr):
        def core_sent(i):
            at = CHIPS - 1 - i
            remote(t1.at[at], r1.at[at], t1_s.at[m, at], t1_r.at[m, at], sib).wait_send()

        loop(0, CHIPS - chip - k, core_sent)

        def chip_sent(i):
            at = CHIPS - 1 - i

            @pl.when(at % PLANE != p)
            def _():
                remote(
                    t2.at[at], r2.at[at], t2_s.at[m, at], t2_r.at[m, at], plane(at % PLANE)
                ).wait_send()

        loop(0, CHIPS - 1 - chip, chip_sent)

        @pl.when(zh == 0)
        def _():
            remote(xs, xr, z_s.at[m], z_r.at[m], far).wait_send()

    def band_send(m, wq, rq):
        for d in range(1, COLS):
            to = (c + d) % COLS
            remote(wq.at[to], rq.at[c], q_s.at[m, to], q_r.at[m, c], in_band(to)).start()

    def band_sum(m, acc, wq, rq):
        for d in range(1, COLS):
            at = (c + d) % COLS
            remote(wq.at[at], rq.at[at], q_s.at[m, at], q_r.at[m, at], in_band(at)).wait_recv()
            acc[...] += rq[at].astype(F32)

    def band_done(m, wq, rq):
        for d in range(1, COLS):
            at = (c + d) % COLS
            remote(wq.at[at], rq.at[at], q_s.at[m, at], q_r.at[m, at], in_band(at)).wait_send()

    cross = 32 + p * 2 + k
    place = (x, y)

    def line_of(half, i):
        return y * SIDE + i if half == 0 else i * SIDE + x

    def gather_copy(n, send, recv, at, device):
        block = gath.at[at]
        return remote(block, block, send, recv, device)

    def half_copy(n, half, send, recv, at, device):
        block = raw.at[n, at, pl.ds(half * HALF, HALF)]
        return remote(block, block, send, recv, device)

    def first_copy(n, half, i, source, device):
        at = line_of(half, source)
        return half_copy(n, half, c_s.at[n, half, i], c_r.at[n, half, source], at, plane(device))

    def second_copy(n, half, e, d):
        source = line_of(half, (place[half] + e) % SIDE)
        to = line_of(1 - half, (place[1 - half] + d) % SIDE)
        return half_copy(
            n, half, c2_s.at[n, half, e, d], c2_r.at[n, half, source], source, plane(to)
        )

    def band_copy(n, to, source, device):
        block = band_raw.at[n, source]
        return remote(block, block, b_s.at[n, to], b_r.at[n, source], in_band(device))

    def far_copy(n):
        return remote(band_raw.at[n, c], raw.at[n, p], x_s.at[n], x_r.at[n], far)

    def own_copy(n, to, source, at, device):
        return gather_copy(n, g_s.at[n, to], g_r.at[n, source], at, plane(device))

    def core_copy(n, at):
        return gather_copy(n, f_s.at[n, at], f_r.at[n, at], at, sib)

    def gather_far(n):
        @pl.when(zh == 1)
        def _():
            far_copy(n).start()

    def gather_band(n):
        for d in range(1, COLS):
            to = (c + d) % COLS
            band_copy(n, to, c, to).start()

    def gather_own(n):
        loop(1, p + 1, lambda i: own_copy(n, p - i, p, r, p - i).start())

        @pl.when(k == 1)
        def _():
            core_copy(n, r).start()

    def probe_of(line, block):
        return (line * nn(inverse[...], block, HIGH)).astype(BF16)

    def gather_first(n):
        @pl.when(zh == 0)
        def _():
            far_copy(n).wait_recv()
            for half in range(2):
                for d in range(1, SIDE):
                    to = (place[half] + d) % SIDE
                    first_copy(n, half, to, place[half], line_of(half, to)).start()
            for half in range(2):
                for d in range(1, SIDE):
                    second_copy(n, half, 0, d).start()

    def gather_second(n):
        @pl.when(zh == 0)
        def _():
            for e in range(1, SIDE):
                for half in range(2):
                    source = (place[half] + e) % SIDE
                    first_copy(n, half, source, source, line_of(half, source)).wait_recv()
                    for d in range(1, SIDE):
                        second_copy(n, half, e, d).start()

    def pass_own(n):
        def own_pass(i):
            at = zh * 32 + i * 2 + k
            own_copy(n, i, i, at, i).wait_recv()
            core_copy(n, at).start()

        loop(p + 1, PLANE, own_pass)

    def pass_cross(n):
        @pl.when(zh == 0)
        def _():
            def cross_pass(i):
                source = (p + i) % PLANE
                at = 32 + source * 2 + k
                for half, same in ((0, source // SIDE == y), (1, source % SIDE == x)):

                    @pl.when(jnp.logical_not(same))
                    def _():
                        half_copy(
                            n,
                            half,
                            c2_s.at[n, half, 0, 0],
                            c2_r.at[n, half, source],
                            source,
                            plane(source),
                        ).wait_recv()

                gath[at] = probe_of(cross_lines[source], raw[n, source])
                core_copy(n, at).start()

            loop(0, PLANE, cross_pass)

    def gather_wait(n):
        loop(p + k, PLANE, lambda i: core_copy(n, zh * 32 + i * 2 + 1 - k).wait_recv())

        @pl.when(zh == 0)
        def _():
            loop(0, PLANE, lambda i: core_copy(n, 32 + i * 2 + 1 - k).wait_recv())

    def gather_z_done(n):
        for d in range(1, COLS):
            to = (c + d) % COLS
            band_copy(n, to, c, to).wait_send()

        @pl.when(zh == 1)
        def _():
            far_copy(n).wait_send()

        @pl.when(zh == 0)
        def _():
            for half in range(2):
                for d in range(1, SIDE):
                    to = (place[half] + d) % SIDE
                    first_copy(n, half, to, place[half], line_of(half, to)).wait_send()
                    for e in range(SIDE):
                        second_copy(n, half, e, d).wait_send()

    def gather_done(n):
        loop(0, p, lambda i: own_copy(n, i, p, r, i).wait_send())

        @pl.when(k == 1)
        def _():
            core_copy(n, r).wait_send()

        loop(p + 1, PLANE, lambda i: core_copy(n, zh * 32 + i * 2 + k).wait_send())

        @pl.when(zh == 0)
        def _():
            loop(0, PLANE, lambda i: core_copy(n, 32 + i * 2 + k).wait_send())

    hole = holes[...]
    onehot = jnp.where(
        lax.broadcasted_iota(jnp.int32, (codes.shape[0], BLK), 0) == hole, 1.0, 0.0
    ).astype(F32)
    start = lax.dot_general(
        codes[...], onehot, (((0,), (0,)), ((), ())), preferred_element_type=F32, precision=HIGH
    )
    band_raw[0, c] = start
    inverse[...] = jnp.where(
        lax.broadcasted_iota(jnp.int32, (K, K), 0) == lax.broadcasted_iota(jnp.int32, (K, K), 1),
        1.0,
        0.0,
    ).astype(F32)
    pl.semaphore_wait(barrier, 1 + PLANE - 1 + 2 * COLS - 1)
    gather_far(0)
    gather_band(0)

    ones = jnp.ones((8, BLK), BF16)
    for i in range(parts):
        loads[i].wait()

        def sums(g):
            slots = [g * SUMS + u for u in range(SUMS)]
            down = [nn(ones, vals[s])[0:1] for s in slots]
            across = [nt(ones, vals[s])[0:1] for s in slots]
            for u, s in enumerate(slots):
                deg_c[s + 1] = deg_c[idx[PREV_COL + s]] + down[u]
                deg_f[s + 1] = deg_f[idx[PREV_ROW + s]] + across[u]

        loop(i * part // SUMS, (i + 1) * part // SUMS, sums)
    near_load.wait()

    mirror_core(0, deg_c, dt1, dr1)
    own_sum = jnp.zeros((1, BLK), F32)
    for q in range(COLS):
        tile = near[:, q * BLK : (q + 1) * BLK]
        own_sum = own_sum + nt(ones, tile)[0:1]
        dwq[q] = deg_f[idx[LAST_ROW + q]] + nn(ones, tile)[0:1]
    dacc[...] = own_sum + dwq[c]
    band_send(0, dwq, drq)
    mirror_plane(0, deg_c, dt1, dr1, dt2, dr2)
    gather_first(0)
    mirror_cross(0, dr2, dt2, dxs, dxr)
    gather_second(0)
    band_sum(0, dacc, dwq, drq)
    mirror_sum(0, dacc, dt1, dr1, dt2, dr2, dxs, dxr)
    scale = 1.0 / jnp.sqrt(dacc[...])

    def line_far():
        return remote(band_lines.at[c], cross_lines.at[p], lx_s.at[0], lx_r.at[0], far)

    def line_band(to, source, device):
        block = band_lines.at[source]
        return remote(block, block, lb_s.at[to], lb_r.at[source], in_band(device))

    band_lines[c] = scale
    for d in range(1, COLS):
        to = (c + d) % COLS
        line_band(to, c, to).start()

    @pl.when(zh == 1)
    def _():
        line_far().start()

    mirror_done(0, dt1, dr1, dt2, dr2, dxs, dxr)
    band_done(0, dwq, drq)
    for d in range(1, COLS):
        at = (c + d) % COLS
        line_band(at, at, at).wait_recv()

    def line_plane(to, source, device):
        block = cross_lines.at[source]
        return remote(block, block, lc_s.at[to], lc_r.at[source], plane(device))

    @pl.when(zh == 0)
    def _():
        line_far().wait_recv()

        def to_plane(i):
            to = (p + i) % PLANE
            line_plane(to, p, to).start()

        loop(1, PLANE, to_plane)

    def lines_wait():
        @pl.when(zh == 0)
        def _():
            def arrived(i):
                source = (p + i) % PLANE
                line_plane(source, source, source).wait_recv()

            loop(1, PLANE, arrived)

    def sweep(it):
        for d in range(1, COLS):
            at = (c + d) % COLS
            band_copy(it, at, at, at).wait_recv()
        for q in range(COLS):
            band[q] = probe_of(band_lines[q], band_raw[it, q])
        gath[r] = band[c]
        gather_own(it)

        def backward(g):
            slots = [g * GROUP + u for u in range(GROUP)]
            tiles = [nn(band[idx[ROW + s]], vals[s]) for s in slots]
            for s, tile in zip(slots, tiles):
                chain_c[s + 1] = chain_c[idx[PREV_COL + s]] + tile

        loop(0, SLOTS // GROUP, backward)
        mirror_core(1, chain_c, t1, r1)

        own = jnp.zeros((K, BLK), F32)
        for q in range(COLS):
            own = own + nt(band[q], near[:, q * BLK : (q + 1) * BLK])
        acc[...] = own

        mirror_plane(1, chain_c, t1, r1, t2, r2)

        pass_own(it)
        pl.when(it == 0)(lines_wait)
        pass_cross(it)
        gather_wait(it)

        mirror_cross(1, r2, t2, xs, xr)

        def forward(g):
            slots = [g * GROUP + u for u in range(GROUP)]
            tiles = [nt(gath[idx[COL + s]], vals[s]) for s in slots]
            for s, tile in zip(slots, tiles):
                chain_f[s + 1] = chain_f[idx[PREV_ROW + s]] + tile

        loop(0, SLOTS // GROUP, forward)
        probe = band[c]
        for q in range(COLS):
            total = chain_f[idx[LAST_ROW + q]] + nn(probe, near[:, q * BLK : (q + 1) * BLK])
            wq[q] = total.astype(BF16)

            @pl.when(c == q)
            def _():
                acc[...] += total

        band_send(1, wq, rq)
        gather_done(it)
        band_sum(1, acc, wq, rq)
        mirror_sum(1, acc, t1, r1, t2, r2, xs, xr)

        image = scale * acc[...]
        more = it < ITERS - 1

        @pl.when(more)
        def _():
            band_raw[it + 1, c] = image
            gather_far(it + 1)

        def when_more(stage):
            pl.when(more)(lambda: stage(it + 1))

        gram = nt(image, image, HIGH)

        low = jnp.concatenate([gram[0:16], gram[16:32]], axis=1)
        high = jnp.concatenate([gram[32:48], gram[48:64]], axis=1)
        gram_send[it] = jnp.where(k == 0, high, low)
        core = remote(gram_send.at[it], gram_core.at[it], a1_s.at[it], a1_r.at[it], sib)
        core.start()
        core.wait_recv()
        gram_plane[it, p] = jnp.where(k == 0, low, high) + gram_core[it]

        def plane_copy(to, source, device):
            block = gram_plane.at[it, source]
            return remote(block, block, a2_s.at[it, to], a2_r.at[it, source], plane(device))

        def plane_start(i):
            to = (p + i) % PLANE
            plane_copy(to, p, to).start()

        loop(1, PLANE, plane_start)

        def plane_wait(i):
            source = (p + i) % PLANE
            plane_copy(source, source, source).wait_recv()

        loop(1, PLANE, plane_wait)
        total = gram_plane[it, 0]
        for i in range(1, PLANE):
            total = total + gram_plane[it, i]
        gram_z[it, z] = total

        def z_copy(to, source, device):
            block = gram_z.at[it, source]
            return remote(block, block, a3_s.at[it, to], a3_r.at[it, source], along_z(device))

        for d in range(1, 2 * COLS):
            to = (z + d) % (2 * COLS)
            z_copy(to, z, to).start()
        when_more(gather_band)
        when_more(gather_first)
        for d in range(1, 2 * COLS):
            at = (z + d) % (2 * COLS)
            z_copy(at, at, at).wait_recv()
        total = gram_z[it, 0]
        for i in range(1, 2 * COLS):
            total = total + gram_z[it, i]
        gram_back[it, k] = total

        def back_copy(half):
            block = gram_back.at[it, half]
            return remote(block, block, a4_s.at[it], a4_r.at[it, half], sib)

        back_copy(k).start()
        when_more(gather_second)
        back_copy(1 - k).wait_recv()
        low = gram_back[it, 0]
        high = gram_back[it, 1]
        gram = jnp.concatenate([low[:, :K], low[:, K:], high[:, :K], high[:, K:]], axis=0)
        total_rows = BLK * BANDS * COLS
        inverse[...] = inverse_factor(gram * (1.0 / total_rows))

        @pl.when(it == ITERS - 1)
        def _():
            out[...] = nn(inverse[...], image, HIGH).T

        mirror_done(1, t1, r1, t2, r2, xs, xr)
        band_done(1, wq, rq)
        core.wait_send()

        def plane_done(i):
            to = (p + i) % PLANE
            plane_copy(to, p, to).wait_send()

        loop(1, PLANE, plane_done)
        for d in range(1, 2 * COLS):
            to = (z + d) % (2 * COLS)
            z_copy(to, z, to).wait_send()
        back_copy(k).wait_send()
        gather_z_done(it)

    loop(0, ITERS, sweep)
    for d in range(1, COLS):
        to = (c + d) % COLS
        line_band(to, c, to).wait_send()

    @pl.when(zh == 1)
    def _():
        line_far().wait_send()

    @pl.when(zh == 0)
    def _():
        def line_sent(i):
            to = (p + i) % PLANE
            line_plane(to, p, to).wait_send()

        loop(1, PLANE, line_sent)


def shards(block_rows, block_cols, block_values, near_values, hole_ids, start_codes):
    row_index = lax.axis_index("row")
    rows = block_rows.reshape(SLOTS)
    cols = block_cols.reshape(SLOTS)
    live = rows >= 0
    local_row = jnp.where(live, rows - row_index * COLS, -1)
    local_col = jnp.where(live, cols // COLS, -1)
    slot = jnp.arange(SLOTS, dtype=jnp.int32)

    def previous(keys):
        same = (keys[None, :] == keys[:, None]) & (slot[None, :] < slot[:, None])
        return jnp.max(jnp.where(same, slot[None, :] + 1, 0), axis=1)

    def last(keys):
        same = keys[None, :] == slot[:, None]
        return jnp.max(jnp.where(same, slot[None, :] + 1, 0), axis=1)

    idx = jnp.concatenate(
        [
            jnp.maximum(local_row, 0),
            jnp.maximum(local_col, 0),
            previous(local_col),
            previous(local_row),
            last(local_col),
            last(local_row),
        ]
    ).astype(jnp.int32)
    block = (K, BLK)
    line = (1, BLK)
    dma = pltpu.SemaphoreType.DMA
    return pl.pallas_call(
        kernel,
        name="subspace",
        out_shape=jax.ShapeDtypeStruct((BLK, K), F32),
        in_specs=[
            pl.BlockSpec(memory_space=pltpu.SMEM),
            pl.BlockSpec(memory_space=pl.ANY),
            pl.BlockSpec(memory_space=pl.ANY),
            pl.BlockSpec(memory_space=pltpu.VMEM),
            pl.BlockSpec(memory_space=pltpu.VMEM),
        ],
        out_specs=pl.BlockSpec(memory_space=pltpu.VMEM),
        scratch_shapes=[
            pltpu.VMEM((SLOTS, BLK, BLK), BF16),
            pltpu.VMEM((BLK, COLS * BLK), BF16),
            pltpu.VMEM((ITERS, PLANE, *block), F32),
            pltpu.VMEM((ITERS, COLS, *block), F32),
            pltpu.VMEM((PLANE, *line), F32),
            pltpu.VMEM((COLS, *line), F32),
            pltpu.VMEM((BANDS, *block), BF16),
            pltpu.VMEM((COLS, *block), BF16),
            pltpu.VMEM((SLOTS + 1, *block), F32),
            pltpu.VMEM((SLOTS + 1, *block), F32),
            pltpu.VMEM((SLOTS + 1, *line), F32),
            pltpu.VMEM((SLOTS + 1, *line), F32),
            pltpu.VMEM((CHIPS, *block), BF16),
            pltpu.VMEM((CHIPS, *block), BF16),
            pltpu.VMEM((CHIPS, *block), BF16),
            pltpu.VMEM((CHIPS, *block), BF16),
            pltpu.VMEM(block, F32),
            pltpu.VMEM(block, F32),
            pltpu.VMEM((COLS, *block), BF16),
            pltpu.VMEM((COLS, *block), BF16),
            pltpu.VMEM((CHIPS, *line), F32),
            pltpu.VMEM((CHIPS, *line), F32),
            pltpu.VMEM((CHIPS, *line), F32),
            pltpu.VMEM((CHIPS, *line), F32),
            pltpu.VMEM(line, F32),
            pltpu.VMEM(line, F32),
            pltpu.VMEM((COLS, *line), F32),
            pltpu.VMEM((COLS, *line), F32),
            pltpu.VMEM(block, F32),
            pltpu.VMEM(line, F32),
            pltpu.VMEM((K, K), F32),
            pltpu.VMEM((ITERS, 16, 2 * K), F32),
            pltpu.VMEM((ITERS, 16, 2 * K), F32),
            pltpu.VMEM((ITERS, PLANE, 16, 2 * K), F32),
            pltpu.VMEM((ITERS, 2 * COLS, 16, 2 * K), F32),
            pltpu.VMEM((ITERS, 2, 16, 2 * K), F32),
            dma((5,)),
            dma((ITERS, PLANE)),
            dma((ITERS, PLANE)),
            dma((ITERS, 2, SIDE)),
            dma((ITERS, 2, SIDE)),
            dma((ITERS,)),
            dma((ITERS,)),
            dma((ITERS, 2, SIDE, SIDE)),
            dma((ITERS, 2, PLANE)),
            dma((ITERS, BANDS)),
            dma((ITERS, BANDS)),
            dma((ITERS, COLS)),
            dma((ITERS, COLS)),
            dma((COLS,)),
            dma((COLS,)),
            dma((1,)),
            dma((1,)),
            dma((PLANE,)),
            dma((PLANE,)),
            dma((2, CHIPS)),
            dma((2, CHIPS)),
            dma((2, CHIPS)),
            dma((2, CHIPS)),
            dma((2,)),
            dma((2,)),
            dma((2, COLS)),
            dma((2, COLS)),
            dma((ITERS,)),
            dma((ITERS,)),
            dma((ITERS, PLANE)),
            dma((ITERS, PLANE)),
            dma((ITERS, 2 * COLS)),
            dma((ITERS, 2 * COLS)),
            dma((ITERS,)),
            dma((ITERS, 2)),
        ],
        compiler_params=pltpu.CompilerParams(
            collective_id=0, has_side_effects=True, vmem_limit_bytes=56 << 20
        ),
    )(
        idx,
        block_values.reshape(SLOTS, BLK, BLK),
        near_values,
        hole_ids.reshape(1, BLK),
        start_codes,
    )


def solution(mesh):
    return jax.shard_map(
        shards,
        mesh=mesh,
        in_specs=(
            P("row", "col", None),
            P("row", "col", None),
            P("row", "col", None, None, None),
            P(("row", "col"), None),
            P(("row", "col")),
            P(),
        ),
        out_specs=P(("row", "col"), None),
        check_vma=False,
    )
```

```python
import jax
import jax.numpy as jnp
from jax import lax
from jax.experimental import pallas as pl
from jax.experimental.pallas import tpu as pltpu
from jax.sharding import PartitionSpec as P

ITERS = 3
MESH = pl.DeviceIdType.MESH
F32 = jnp.float32
BF16 = jnp.bfloat16
HIGH = lax.Precision.HIGHEST

SLOTS = 64
BLK = 256
K = 64
BANDS = 64
CHIPS = 32
PLANE = 16
COLS = 4
SIDE = 4
HALF = K // 2
TILE = 8
GROUP = 32
SUMS = 16

ROW, COL, PREV_COL, PREV_ROW, LAST_COL, LAST_ROW = (i * SLOTS for i in range(6))


def remote(src, dst, send_sem, recv_sem, device):
    return pltpu.make_async_remote_copy(
        src_ref=src,
        dst_ref=dst,
        send_sem=send_sem,
        recv_sem=recv_sem,
        device_id=device,
        device_id_type=MESH,
    )


def nt(a, b, precision=None):
    return lax.dot_general(
        a, b, (((1,), (1,)), ((), ())), preferred_element_type=F32, precision=precision
    )


def nn(a, b, precision=None):
    return lax.dot_general(
        a, b, (((1,), (0,)), ((), ())), preferred_element_type=F32, precision=precision
    )


def loop(first, last, body):
    def step(i, carry):
        body(i)
        return carry

    lax.fori_loop(first, last, step, 0)


def inverse_factor(gram):
    row = lax.broadcasted_iota(jnp.int32, (K, 2 * K), 0)
    lane = lax.broadcasted_iota(jnp.int32, (K, 2 * K), 1)
    sub = lax.broadcasted_iota(jnp.int32, (TILE, 2 * K), 0)
    wide = jnp.concatenate([gram, jnp.zeros((K, K), F32)], axis=1)
    wide = wide + jnp.where(lane == row + K, 1.0, 0.0).astype(F32)
    tiles = [wide[t : t + TILE, :] for t in range(0, K, TILE)]
    for t, tile in enumerate(tiles):
        first = t * TILE
        rows = [tile[i : i + 1, :] for i in range(TILE)]
        entry = {
            (i, m): jnp.broadcast_to(rows[i][:, first + m : first + m + 1], (1, 2 * K))
            for i in range(TILE)
            for m in range(i, TILE)
        }
        later = range(t + 1, K // TILE)
        factor = {
            (u, m): jnp.broadcast_to(tiles[u][:, first + m : first + m + 1], (TILE, 2 * K))
            for u in later
            for m in range(TILE)
        }
        scaled = []
        for i in range(TILE):
            reciprocal = 1.0 / entry[i, i]
            for n in range(i + 1, TILE):
                ratio = entry[i, n] * reciprocal
                rows[n] = rows[n] - ratio * rows[i]
                for m in range(n, TILE):
                    entry[n, m] = entry[n, m] - ratio * entry[i, m]
                for u in later:
                    factor[u, n] = factor[u, n] - ratio * factor[u, i]
            scaled.append(rows[i] * reciprocal)
        for u in later:
            for i in range(TILE):
                tiles[u] = tiles[u] - factor[u, i] * scaled[i]
        for i in range(1, TILE):
            tile = jnp.where(sub == i, rows[i], tile)
        tiles[t] = tile
    done = jnp.concatenate(tiles, axis=0)
    diag = jnp.sum(jnp.where(lane == row, done, 0.0), axis=1, keepdims=True)
    return done[:, K:] / jnp.sqrt(diag)


def kernel(
    idx,
    vals_hbm,
    near_hbm,
    holes,
    codes,
    out,
    vals,
    near,
    raw,
    band_raw,
    cross_lines,
    band_lines,
    gath,
    band,
    chain_c,
    chain_f,
    deg_c,
    deg_f,
    t1,
    r1,
    t2,
    r2,
    xs,
    xr,
    wq,
    rq,
    dt1,
    dr1,
    dt2,
    dr2,
    dxs,
    dxr,
    code_parts,
    hole_band,
    hole_cross,
    dwq,
    drq,
    acc,
    dacc,
    inverse,
    gram_send,
    gram_core,
    gram_plane,
    gram_z,
    gram_back,
    load_sem,
    g_s,
    g_r,
    c_s,
    c_r,
    x_s,
    x_r,
    c2_s,
    c2_r,
    f_s,
    f_r,
    b_s,
    b_r,
    lb_s,
    lb_r,
    lx_s,
    lx_r,
    lc_s,
    lc_r,
    hb_s,
    hb_r,
    hx_s,
    hx_r,
    hc_s,
    hc_r,
    t1_s,
    t1_r,
    t2_s,
    t2_r,
    z_s,
    z_r,
    q_s,
    q_r,
    a1_s,
    a1_r,
    a2_s,
    a2_r,
    a3_s,
    a3_r,
    a4_s,
    a4_r,
):
    r = lax.axis_index("row")
    c = lax.axis_index("col")
    k = r % 2
    chip = r // 2
    p = chip % PLANE
    y = p // SIDE
    x = p % SIDE
    zh = r // 32
    z = zh * COLS + c
    sib = (r + 1 - 2 * k, c)
    far = ((1 - zh) * 32 + p * 2 + k, c)

    def plane(i):
        return (zh * 32 + i * 2 + k, c)

    def in_band(i):
        return (r, i)

    def along_z(i):
        return ((i // COLS) * 32 + p * 2 + k, i % COLS)

    parts = 4
    part = SLOTS // parts
    near_load = pltpu.make_async_copy(near_hbm, near, load_sem.at[parts])
    near_load.start()
    loads = [
        pltpu.make_async_copy(
            vals_hbm.at[pl.ds(i * part, part)], vals.at[pl.ds(i * part, part)], load_sem.at[i]
        )
        for i in range(parts)
    ]
    for load in loads:
        load.start()

    barrier = pltpu.get_barrier_semaphore()
    pl.semaphore_signal(barrier, inc=1, device_id=sib, device_id_type=MESH)
    for d in range(1, PLANE):
        pl.semaphore_signal(
            barrier, inc=1, device_id=plane((p + d) % PLANE), device_id_type=MESH
        )
    for d in range(1, 2 * COLS):
        pl.semaphore_signal(
            barrier, inc=1, device_id=along_z((z + d) % (2 * COLS)), device_id_type=MESH
        )

    chain_c[0] = jnp.zeros((K, BLK), F32)
    chain_f[0] = jnp.zeros((K, BLK), F32)
    deg_c[0] = jnp.zeros((1, BLK), F32)
    deg_f[0] = jnp.zeros((1, BLK), F32)

    def each_later(body, first):
        @pl.when(zh == 0)
        def _():
            loop(1, PLANE + 1, lambda i: body(PLANE + (p + i) % PLANE))

        loop(first, PLANE, lambda i: body(zh * PLANE + i))

    def mirror_core(m, chain, t1, r1):
        kind = t1.dtype

        def to_core(at):
            t1[at] = chain[idx[LAST_COL + at * 2 + 1 - k]].astype(kind)
            remote(t1.at[at], r1.at[at], t1_s.at[m, at], t1_r.at[m, at], sib).start()

        each_later(to_core, p + k)

    def mirror_plane(m, chain, t1, r1, t2, r2):
        kind = t2.dtype

        def to_chip(at):
            to, half = at % PLANE, at // PLANE
            remote(t1.at[at], r1.at[at], t1_s.at[m, at], t1_r.at[m, at], sib).wait_recv()
            both = (chain[idx[LAST_COL + at * 2 + k]] + r1[at].astype(F32)).astype(kind)

            @pl.when(to == p)
            def _():
                r2[PLANE + p] = both

            @pl.when(to != p)
            def _():
                t2[at] = both
                remote(
                    t2.at[at],
                    r2.at[half * PLANE + p],
                    t2_s.at[m, at],
                    t2_r.at[m, half * PLANE + p],
                    plane(to),
                ).start()

        each_later(to_chip, p + 1)

    def mirror_cross(m, r2, t2, xs, xr):
        @pl.when(zh == 0)
        def _():
            def add(i, total):
                source = (p + i) % PLANE
                at = PLANE + source
                remote(t2.at[at], r2.at[at], t2_s.at[m, at], t2_r.at[m, at], plane(source)).wait_recv()
                return total + r2[at].astype(F32)

            xs[...] = lax.fori_loop(1, PLANE, add, r2[PLANE + p].astype(F32))
            remote(xs, xr, z_s.at[m], z_r.at[m], far).start()

    def mirror_sum(m, acc, t1, r1, t2, r2, xs, xr):
        def add(i, total):
            at = zh * PLANE + i
            remote(t2.at[at], r2.at[at], t2_s.at[m, at], t2_r.at[m, at], plane(i)).wait_recv()
            return total + r2[at].astype(F32)

        acc[...] += lax.fori_loop(0, p, add, jnp.zeros(acc.shape, F32))

        @pl.when(k == 1)
        def _():
            remote(
                t1.at[chip], r1.at[chip], t1_s.at[m, chip], t1_r.at[m, chip], sib
            ).wait_recv()
            acc[...] += r1[chip].astype(F32)

        @pl.when(zh == 1)
        def _():
            remote(xs, xr, z_s.at[m], z_r.at[m], far).wait_recv()
            acc[...] += xr[...]

    def mirror_done(m, t1, r1, t2, r2, xs, xr):
        def core_sent(i):
            at = CHIPS - 1 - i
            remote(t1.at[at], r1.at[at], t1_s.at[m, at], t1_r.at[m, at], sib).wait_send()

        loop(0, CHIPS - chip - k, core_sent)

        def chip_sent(i):
            at = CHIPS - 1 - i

            @pl.when(at % PLANE != p)
            def _():
                remote(
                    t2.at[at], r2.at[at], t2_s.at[m, at], t2_r.at[m, at], plane(at % PLANE)
                ).wait_send()

        loop(0, CHIPS - 1 - chip, chip_sent)

        @pl.when(zh == 0)
        def _():
            remote(xs, xr, z_s.at[m], z_r.at[m], far).wait_send()

    def band_send(m, wq, rq):
        for d in range(1, COLS):
            to = (c + d) % COLS
            remote(wq.at[to], rq.at[c], q_s.at[m, to], q_r.at[m, c], in_band(to)).start()

    def band_sum(m, acc, wq, rq):
        for d in range(1, COLS):
            at = (c + d) % COLS
            remote(wq.at[at], rq.at[at], q_s.at[m, at], q_r.at[m, at], in_band(at)).wait_recv()
            acc[...] += rq[at].astype(F32)

    def band_done(m, wq, rq):
        for d in range(1, COLS):
            at = (c + d) % COLS
            remote(wq.at[at], rq.at[at], q_s.at[m, at], q_r.at[m, at], in_band(at)).wait_send()

    cross = 32 + p * 2 + k
    place = (x, y)

    def line_of(half, i):
        return y * SIDE + i if half == 0 else i * SIDE + x

    def gather_copy(n, send, recv, at, device):
        block = gath.at[at]
        return remote(block, block, send, recv, device)

    def half_copy(n, half, send, recv, at, device):
        block = raw.at[n, at, pl.ds(half * HALF, HALF)]
        return remote(block, block, send, recv, device)

    def first_copy(n, half, i, source, device):
        at = line_of(half, source)
        return half_copy(n, half, c_s.at[n, half, i], c_r.at[n, half, source], at, plane(device))

    def second_copy(n, half, e, d):
        source = line_of(half, (place[half] + e) % SIDE)
        to = line_of(1 - half, (place[1 - half] + d) % SIDE)
        return half_copy(
            n, half, c2_s.at[n, half, e, d], c2_r.at[n, half, source], source, plane(to)
        )

    def band_copy(n, to, source, device):
        block = band_raw.at[n, source]
        return remote(block, block, b_s.at[n, to], b_r.at[n, source], in_band(device))

    def far_copy(n):
        return remote(band_raw.at[n, c], raw.at[n, p], x_s.at[n], x_r.at[n], far)

    def own_copy(n, to, source, at, device):
        return gather_copy(n, g_s.at[n, to], g_r.at[n, source], at, plane(device))

    def core_copy(n, at):
        return gather_copy(n, f_s.at[n, at], f_r.at[n, at], at, sib)

    def gather_far(n):
        @pl.when(zh == 1)
        def _():
            far_copy(n).start()

    def gather_band(n):
        for d in range(1, COLS):
            to = (c + d) % COLS
            band_copy(n, to, c, to).start()

    def gather_own(n):
        loop(1, p + 1, lambda i: own_copy(n, p - i, p, r, p - i).start())

        @pl.when(k == 1)
        def _():
            core_copy(n, r).start()

    def probe_of(line, block):
        return (line * nn(inverse[...], block, HIGH)).astype(BF16)

    def gather_first(n):
        @pl.when(zh == 0)
        def _():
            far_copy(n).wait_recv()
            for half in range(2):
                for d in range(1, SIDE):
                    to = (place[half] + d) % SIDE
                    first_copy(n, half, to, place[half], line_of(half, to)).start()
            for half in range(2):
                for d in range(1, SIDE):
                    second_copy(n, half, 0, d).start()

    def gather_second(n):
        @pl.when(zh == 0)
        def _():
            for e in range(1, SIDE):
                for half in range(2):
                    source = (place[half] + e) % SIDE
                    first_copy(n, half, source, source, line_of(half, source)).wait_recv()
                    for d in range(1, SIDE):
                        second_copy(n, half, e, d).start()

    def pass_own(n):
        def own_pass(i):
            at = zh * 32 + i * 2 + k
            own_copy(n, i, i, at, i).wait_recv()
            core_copy(n, at).start()

        loop(p + 1, PLANE, own_pass)

    def pass_cross(n):
        @pl.when(zh == 0)
        def _():
            def cross_pass(i):
                source = (p + i) % PLANE
                at = 32 + source * 2 + k
                for half, same in ((0, source // SIDE == y), (1, source % SIDE == x)):

                    @pl.when(jnp.logical_and(n > 0, jnp.logical_not(same)))
                    def _():
                        half_copy(
                            n,
                            half,
                            c2_s.at[n, half, 0, 0],
                            c2_r.at[n, half, source],
                            source,
                            plane(source),
                        ).wait_recv()

                gath[at] = probe_of(cross_lines[source], raw[n, source])
                core_copy(n, at).start()

            loop(0, PLANE, cross_pass)

    def gather_wait(n):
        loop(p + k, PLANE, lambda i: core_copy(n, zh * 32 + i * 2 + 1 - k).wait_recv())

        @pl.when(zh == 0)
        def _():
            loop(0, PLANE, lambda i: core_copy(n, 32 + i * 2 + 1 - k).wait_recv())

    def gather_z_done(n):
        for d in range(1, COLS):
            to = (c + d) % COLS
            band_copy(n, to, c, to).wait_send()

        @pl.when(zh == 1)
        def _():
            far_copy(n).wait_send()

        @pl.when(zh == 0)
        def _():
            for half in range(2):
                for d in range(1, SIDE):
                    to = (place[half] + d) % SIDE
                    first_copy(n, half, to, place[half], line_of(half, to)).wait_send()
                    for e in range(SIDE):
                        second_copy(n, half, e, d).wait_send()

    def gather_done(n):
        loop(0, p, lambda i: own_copy(n, i, p, r, i).wait_send())

        @pl.when(k == 1)
        def _():
            core_copy(n, r).wait_send()

        loop(p + 1, PLANE, lambda i: core_copy(n, zh * 32 + i * 2 + k).wait_send())

        @pl.when(zh == 0)
        def _():
            loop(0, PLANE, lambda i: core_copy(n, 32 + i * 2 + k).wait_send())

    code_high = codes[...].astype(BF16)
    code_rest = codes[...] - code_high.astype(F32)
    code_middle = code_rest.astype(BF16)
    code_low = (code_rest - code_middle.astype(F32)).astype(BF16)
    code_parts[...] = jnp.concatenate([code_high, code_middle, code_low], axis=0)

    def start_of(hole):
        onehot = jnp.where(
            lax.broadcasted_iota(jnp.int32, (codes.shape[1], BLK), 0) == hole, 1.0, 0.0
        ).astype(BF16)
        picked = nn(code_parts[...], onehot)
        return picked[:K] + picked[K : 2 * K] + picked[2 * K :]

    def hole_band_copy(to, source, device):
        return remote(
            holes, hole_band.at[source], hb_s.at[to], hb_r.at[source], in_band(device)
        )

    def hole_far_copy():
        return remote(holes, hole_cross.at[p], hx_s.at[0], hx_r.at[0], far)

    def hole_plane_copy(to, source, device):
        block = hole_cross.at[source]
        return remote(block, block, hc_s.at[to], hc_r.at[source], plane(device))

    band_raw[0, c] = start_of(holes[...])
    inverse[...] = jnp.where(
        lax.broadcasted_iota(jnp.int32, (K, K), 0) == lax.broadcasted_iota(jnp.int32, (K, K), 1),
        1.0,
        0.0,
    ).astype(F32)

    ones = jnp.ones((8, BLK), BF16)
    for i in range(parts):
        loads[i].wait()

        def sums(g):
            slots = [g * SUMS + u for u in range(SUMS)]
            down = [nn(ones, vals[s])[0:1] for s in slots]
            across = [nt(ones, vals[s])[0:1] for s in slots]
            for u, s in enumerate(slots):
                deg_c[s + 1] = deg_c[idx[PREV_COL + s]] + down[u]
                deg_f[s + 1] = deg_f[idx[PREV_ROW + s]] + across[u]

        loop(i * part // SUMS, (i + 1) * part // SUMS, sums)
    near_load.wait()
    pl.semaphore_wait(barrier, 1 + PLANE - 1 + 2 * COLS - 1)
    for d in range(1, COLS):
        to = (c + d) % COLS
        hole_band_copy(to, c, to).start()

    @pl.when(zh == 1)
    def _():
        hole_far_copy().start()


    mirror_core(0, deg_c, dt1, dr1)
    own_sum = jnp.zeros((1, BLK), F32)
    for q in range(COLS):
        tile = near[:, q * BLK : (q + 1) * BLK]
        own_sum = own_sum + nt(ones, tile)[0:1]
        dwq[q] = deg_f[idx[LAST_ROW + q]] + nn(ones, tile)[0:1]
    dacc[...] = own_sum + dwq[c]
    band_send(0, dwq, drq)
    mirror_plane(0, deg_c, dt1, dr1, dt2, dr2)

    @pl.when(zh == 0)
    def _():
        hole_far_copy().wait_recv()

        def hole_start(i):
            to = (p + i) % PLANE
            hole_plane_copy(to, p, to).start()

        loop(1, PLANE, hole_start)

    for d in range(1, COLS):
        at = (c + d) % COLS
        hole_band_copy(at, at, at).wait_recv()
        band_raw[0, at] = start_of(hole_band[at])
    mirror_cross(0, dr2, dt2, dxs, dxr)
    band_sum(0, dacc, dwq, drq)
    mirror_sum(0, dacc, dt1, dr1, dt2, dr2, dxs, dxr)
    scale = 1.0 / jnp.sqrt(dacc[...])

    def line_far():
        return remote(band_lines.at[c], cross_lines.at[p], lx_s.at[0], lx_r.at[0], far)

    def line_band(to, source, device):
        block = band_lines.at[source]
        return remote(block, block, lb_s.at[to], lb_r.at[source], in_band(device))

    band_lines[c] = scale
    for d in range(1, COLS):
        to = (c + d) % COLS
        line_band(to, c, to).start()

    @pl.when(zh == 1)
    def _():
        line_far().start()

    @pl.when(zh == 0)
    def _():
        raw[0, p] = start_of(hole_cross[p])

        def hole_wait(i):
            source = (p + i) % PLANE
            hole_plane_copy(source, source, source).wait_recv()
            raw[0, source] = start_of(hole_cross[source])

        loop(1, PLANE, hole_wait)

    mirror_done(0, dt1, dr1, dt2, dr2, dxs, dxr)
    band_done(0, dwq, drq)
    for d in range(1, COLS):
        at = (c + d) % COLS
        line_band(at, at, at).wait_recv()

    def line_plane(to, source, device):
        block = cross_lines.at[source]
        return remote(block, block, lc_s.at[to], lc_r.at[source], plane(device))

    @pl.when(zh == 0)
    def _():
        line_far().wait_recv()

        def to_plane(i):
            to = (p + i) % PLANE
            line_plane(to, p, to).start()

        loop(1, PLANE, to_plane)

    def lines_wait():
        @pl.when(zh == 0)
        def _():
            def arrived(i):
                source = (p + i) % PLANE
                line_plane(source, source, source).wait_recv()

            loop(1, PLANE, arrived)

    def sweep(it):
        @pl.when(it > 0)
        def _():
            for d in range(1, COLS):
                at = (c + d) % COLS
                band_copy(it, at, at, at).wait_recv()

        for q in range(COLS):
            band[q] = probe_of(band_lines[q], band_raw[it, q])
        gath[r] = band[c]
        gather_own(it)

        def backward(g):
            slots = [g * GROUP + u for u in range(GROUP)]
            tiles = [nn(band[idx[ROW + s]], vals[s]) for s in slots]
            for s, tile in zip(slots, tiles):
                chain_c[s + 1] = chain_c[idx[PREV_COL + s]] + tile

        loop(0, SLOTS // GROUP, backward)
        mirror_core(1, chain_c, t1, r1)

        own = jnp.zeros((K, BLK), F32)
        for q in range(COLS):
            own = own + nt(band[q], near[:, q * BLK : (q + 1) * BLK])
        acc[...] = own

        mirror_plane(1, chain_c, t1, r1, t2, r2)

        pass_own(it)
        pl.when(it == 0)(lines_wait)
        pass_cross(it)
        gather_wait(it)

        mirror_cross(1, r2, t2, xs, xr)

        def forward(g):
            slots = [g * GROUP + u for u in range(GROUP)]
            tiles = [nt(gath[idx[COL + s]], vals[s]) for s in slots]
            for s, tile in zip(slots, tiles):
                chain_f[s + 1] = chain_f[idx[PREV_ROW + s]] + tile

        loop(0, SLOTS // GROUP, forward)
        probe = band[c]
        for q in range(COLS):
            total = chain_f[idx[LAST_ROW + q]] + nn(probe, near[:, q * BLK : (q + 1) * BLK])
            wq[q] = total.astype(BF16)

            @pl.when(c == q)
            def _():
                acc[...] += total

        band_send(1, wq, rq)
        gather_done(it)
        band_sum(1, acc, wq, rq)
        mirror_sum(1, acc, t1, r1, t2, r2, xs, xr)

        image = scale * acc[...]
        more = it < ITERS - 1

        @pl.when(more)
        def _():
            band_raw[it + 1, c] = image
            gather_far(it + 1)

        def when_more(stage):
            pl.when(more)(lambda: stage(it + 1))

        gram = nt(image, image, HIGH)

        low = jnp.concatenate([gram[0:16], gram[16:32]], axis=1)
        high = jnp.concatenate([gram[32:48], gram[48:64]], axis=1)
        gram_send[it] = jnp.where(k == 0, high, low)
        core = remote(gram_send.at[it], gram_core.at[it], a1_s.at[it], a1_r.at[it], sib)
        core.start()
        core.wait_recv()
        gram_plane[it, p] = jnp.where(k == 0, low, high) + gram_core[it]

        def plane_copy(to, source, device):
            block = gram_plane.at[it, source]
            return remote(block, block, a2_s.at[it, to], a2_r.at[it, source], plane(device))

        def plane_start(i):
            to = (p + i) % PLANE
            plane_copy(to, p, to).start()

        loop(1, PLANE, plane_start)

        def plane_wait(i):
            source = (p + i) % PLANE
            plane_copy(source, source, source).wait_recv()

        loop(1, PLANE, plane_wait)
        total = gram_plane[it, 0]
        for i in range(1, PLANE):
            total = total + gram_plane[it, i]
        gram_z[it, z] = total

        def z_copy(to, source, device):
            block = gram_z.at[it, source]
            return remote(block, block, a3_s.at[it, to], a3_r.at[it, source], along_z(device))

        for d in range(1, 2 * COLS):
            to = (z + d) % (2 * COLS)
            z_copy(to, z, to).start()
        when_more(gather_band)
        when_more(gather_first)
        for d in range(1, 2 * COLS):
            at = (z + d) % (2 * COLS)
            z_copy(at, at, at).wait_recv()
        total = gram_z[it, 0]
        for i in range(1, 2 * COLS):
            total = total + gram_z[it, i]
        gram_back[it, k] = total

        def back_copy(half):
            block = gram_back.at[it, half]
            return remote(block, block, a4_s.at[it], a4_r.at[it, half], sib)

        back_copy(k).start()
        when_more(gather_second)
        back_copy(1 - k).wait_recv()
        low = gram_back[it, 0]
        high = gram_back[it, 1]
        gram = jnp.concatenate([low[:, :K], low[:, K:], high[:, :K], high[:, K:]], axis=0)
        total_rows = BLK * BANDS * COLS
        inverse[...] = inverse_factor(gram * (1.0 / total_rows))

        @pl.when(it == ITERS - 1)
        def _():
            out[...] = nn(inverse[...], image, HIGH)

        mirror_done(1, t1, r1, t2, r2, xs, xr)
        band_done(1, wq, rq)
        core.wait_send()

        def plane_done(i):
            to = (p + i) % PLANE
            plane_copy(to, p, to).wait_send()

        loop(1, PLANE, plane_done)
        for d in range(1, 2 * COLS):
            to = (z + d) % (2 * COLS)
            z_copy(to, z, to).wait_send()
        back_copy(k).wait_send()
        pl.when(it > 0)(lambda: gather_z_done(it))

    loop(0, ITERS, sweep)
    for d in range(1, COLS):
        to = (c + d) % COLS
        line_band(to, c, to).wait_send()
        hole_band_copy(to, c, to).wait_send()

    @pl.when(zh == 1)
    def _():
        line_far().wait_send()
        hole_far_copy().wait_send()

    @pl.when(zh == 0)
    def _():
        def line_sent(i):
            to = (p + i) % PLANE
            line_plane(to, p, to).wait_send()
            hole_plane_copy(to, p, to).wait_send()

        loop(1, PLANE, line_sent)


def shards(block_rows, block_cols, block_values, near_values, hole_ids, start_codes):
    row_index = lax.axis_index("row")
    rows = block_rows.reshape(SLOTS)
    cols = block_cols.reshape(SLOTS)
    live = rows >= 0
    local_row = jnp.where(live, rows - row_index * COLS, -1)
    local_col = jnp.where(live, cols // COLS, -1)
    slot = jnp.arange(SLOTS, dtype=jnp.int32)

    def previous(keys):
        same = (keys[None, :] == keys[:, None]) & (slot[None, :] < slot[:, None])
        return jnp.max(jnp.where(same, slot[None, :] + 1, 0), axis=1)

    def last(keys):
        same = keys[None, :] == slot[:, None]
        return jnp.max(jnp.where(same, slot[None, :] + 1, 0), axis=1)

    idx = jnp.concatenate(
        [
            jnp.maximum(local_row, 0),
            jnp.maximum(local_col, 0),
            previous(local_col),
            previous(local_row),
            last(local_col),
            last(local_row),
        ]
    ).astype(jnp.int32)
    block = (K, BLK)
    line = (1, BLK)
    dma = pltpu.SemaphoreType.DMA
    return pl.pallas_call(
        kernel,
        name="subspace",
        out_shape=jax.ShapeDtypeStruct((K, BLK), F32),
        in_specs=[
            pl.BlockSpec(memory_space=pltpu.SMEM),
            pl.BlockSpec(memory_space=pl.ANY),
            pl.BlockSpec(memory_space=pl.ANY),
            pl.BlockSpec(memory_space=pltpu.VMEM),
            pl.BlockSpec(memory_space=pltpu.VMEM),
        ],
        out_specs=pl.BlockSpec(memory_space=pltpu.VMEM),
        scratch_shapes=[
            pltpu.VMEM((SLOTS, BLK, BLK), BF16),
            pltpu.VMEM((BLK, COLS * BLK), BF16),
            pltpu.VMEM((ITERS, PLANE, *block), F32),
            pltpu.VMEM((ITERS, COLS, *block), F32),
            pltpu.VMEM((PLANE, *line), F32),
            pltpu.VMEM((COLS, *line), F32),
            pltpu.VMEM((BANDS, *block), BF16),
            pltpu.VMEM((COLS, *block), BF16),
            pltpu.VMEM((SLOTS + 1, *block), F32),
            pltpu.VMEM((SLOTS + 1, *block), F32),
            pltpu.VMEM((SLOTS + 1, *line), F32),
            pltpu.VMEM((SLOTS + 1, *line), F32),
            pltpu.VMEM((CHIPS, *block), BF16),
            pltpu.VMEM((CHIPS, *block), BF16),
            pltpu.VMEM((CHIPS, *block), BF16),
            pltpu.VMEM((CHIPS, *block), BF16),
            pltpu.VMEM(block, F32),
            pltpu.VMEM(block, F32),
            pltpu.VMEM((COLS, *block), BF16),
            pltpu.VMEM((COLS, *block), BF16),
            pltpu.VMEM((CHIPS, *line), F32),
            pltpu.VMEM((CHIPS, *line), F32),
            pltpu.VMEM((CHIPS, *line), F32),
            pltpu.VMEM((CHIPS, *line), F32),
            pltpu.VMEM(line, F32),
            pltpu.VMEM(line, F32),
            pltpu.VMEM((3 * K, start_codes.shape[0]), BF16),
            pltpu.VMEM((COLS, *line), jnp.int32),
            pltpu.VMEM((PLANE, *line), jnp.int32),
            pltpu.VMEM((COLS, *line), F32),
            pltpu.VMEM((COLS, *line), F32),
            pltpu.VMEM(block, F32),
            pltpu.VMEM(line, F32),
            pltpu.VMEM((K, K), F32),
            pltpu.VMEM((ITERS, 16, 2 * K), F32),
            pltpu.VMEM((ITERS, 16, 2 * K), F32),
            pltpu.VMEM((ITERS, PLANE, 16, 2 * K), F32),
            pltpu.VMEM((ITERS, 2 * COLS, 16, 2 * K), F32),
            pltpu.VMEM((ITERS, 2, 16, 2 * K), F32),
            dma((5,)),
            dma((ITERS, PLANE)),
            dma((ITERS, PLANE)),
            dma((ITERS, 2, SIDE)),
            dma((ITERS, 2, SIDE)),
            dma((ITERS,)),
            dma((ITERS,)),
            dma((ITERS, 2, SIDE, SIDE)),
            dma((ITERS, 2, PLANE)),
            dma((ITERS, BANDS)),
            dma((ITERS, BANDS)),
            dma((ITERS, COLS)),
            dma((ITERS, COLS)),
            dma((COLS,)),
            dma((COLS,)),
            dma((1,)),
            dma((1,)),
            dma((PLANE,)),
            dma((PLANE,)),
            dma((COLS,)),
            dma((COLS,)),
            dma((1,)),
            dma((1,)),
            dma((PLANE,)),
            dma((PLANE,)),
            dma((2, CHIPS)),
            dma((2, CHIPS)),
            dma((2, CHIPS)),
            dma((2, CHIPS)),
            dma((2,)),
            dma((2,)),
            dma((2, COLS)),
            dma((2, COLS)),
            dma((ITERS,)),
            dma((ITERS,)),
            dma((ITERS, PLANE)),
            dma((ITERS, PLANE)),
            dma((ITERS, 2 * COLS)),
            dma((ITERS, 2 * COLS)),
            dma((ITERS,)),
            dma((ITERS, 2)),
        ],
        compiler_params=pltpu.CompilerParams(
            collective_id=0, has_side_effects=True, vmem_limit_bytes=56 << 20
        ),
    )(
        idx,
        block_values.reshape(SLOTS, BLK, BLK),
        near_values,
        hole_ids.reshape(1, BLK),
        start_codes.T,
    ).T


def solution(mesh):
    return jax.shard_map(
        shards,
        mesh=mesh,
        in_specs=(
            P("row", "col", None),
            P("row", "col", None),
            P("row", "col", None, None, None),
            P(("row", "col"), None),
            P(("row", "col")),
            P(),
        ),
        out_specs=P(("row", "col"), None),
        check_vma=False,
    )
```

```python
import jax
import jax.numpy as jnp
from jax import lax
from jax.experimental import pallas as pl
from jax.experimental.pallas import tpu as pltpu
from jax.sharding import PartitionSpec as P

ITERS = 3
MESH = pl.DeviceIdType.MESH
F32 = jnp.float32
BF16 = jnp.bfloat16
HIGH = lax.Precision.HIGHEST

SLOTS = 64
BLK = 256
K = 64
BANDS = 64
CHIPS = 32
PLANE = 16
COLS = 4
SIDE = 4
HALF = K // 2
TILE = 8
GROUP = 32
SUMS = 16

ROW, COL, PREV_COL, PREV_ROW, LAST_COL, LAST_ROW = (i * SLOTS for i in range(6))


def remote(src, dst, send_sem, recv_sem, device):
    return pltpu.make_async_remote_copy(
        src_ref=src,
        dst_ref=dst,
        send_sem=send_sem,
        recv_sem=recv_sem,
        device_id=device,
        device_id_type=MESH,
    )


def nt(a, b, precision=None):
    return lax.dot_general(
        a, b, (((1,), (1,)), ((), ())), preferred_element_type=F32, precision=precision
    )


def nn(a, b, precision=None):
    return lax.dot_general(
        a, b, (((1,), (0,)), ((), ())), preferred_element_type=F32, precision=precision
    )


def loop(first, last, body):
    def step(i, carry):
        body(i)
        return carry

    lax.fori_loop(first, last, step, 0)


def inverse_factor(gram):
    row = lax.broadcasted_iota(jnp.int32, (K, 2 * K), 0)
    lane = lax.broadcasted_iota(jnp.int32, (K, 2 * K), 1)
    sub = lax.broadcasted_iota(jnp.int32, (TILE, 2 * K), 0)
    wide = jnp.concatenate([gram, jnp.zeros((K, K), F32)], axis=1)
    wide = wide + jnp.where(lane == row + K, 1.0, 0.0).astype(F32)
    tiles = [wide[t : t + TILE, :] for t in range(0, K, TILE)]
    for t, tile in enumerate(tiles):
        first = t * TILE
        rows = [tile[i : i + 1, :] for i in range(TILE)]
        entry = {
            (i, m): jnp.broadcast_to(rows[i][:, first + m : first + m + 1], (1, 2 * K))
            for i in range(TILE)
            for m in range(i, TILE)
        }
        later = range(t + 1, K // TILE)
        factor = {
            (u, m): jnp.broadcast_to(tiles[u][:, first + m : first + m + 1], (TILE, 2 * K))
            for u in later
            for m in range(TILE)
        }
        scaled = []
        for i in range(TILE):
            reciprocal = 1.0 / entry[i, i]
            for n in range(i + 1, TILE):
                ratio = entry[i, n] * reciprocal
                rows[n] = rows[n] - ratio * rows[i]
                for m in range(n, TILE):
                    entry[n, m] = entry[n, m] - ratio * entry[i, m]
                for u in later:
                    factor[u, n] = factor[u, n] - ratio * factor[u, i]
            scaled.append(rows[i] * reciprocal)
        for u in later:
            for i in range(TILE):
                tiles[u] = tiles[u] - factor[u, i] * scaled[i]
        for i in range(1, TILE):
            tile = jnp.where(sub == i, rows[i], tile)
        tiles[t] = tile
    done = jnp.concatenate(tiles, axis=0)
    diag = jnp.sum(jnp.where(lane == row, done, 0.0), axis=1, keepdims=True)
    return done[:, K:] / jnp.sqrt(diag)


def kernel(
    idx,
    vals_hbm,
    near_hbm,
    holes,
    codes,
    out,
    vals,
    near,
    raw,
    band_raw,
    cross_lines,
    band_lines,
    gath,
    band,
    chain_c,
    chain_f,
    deg_c,
    deg_f,
    t1,
    r1,
    t2,
    r2,
    xs,
    xr,
    wq,
    rq,
    dt1,
    dr1,
    dt2,
    dr2,
    dxs,
    dxr,
    code_parts,
    hole_band,
    hole_cross,
    dwq,
    drq,
    acc,
    dacc,
    inverse,
    gram_send,
    gram_core,
    gram_plane,
    gram_z,
    gram_back,
    load_sem,
    g_s,
    g_r,
    c_s,
    c_r,
    x_s,
    x_r,
    c2_s,
    c2_r,
    f_s,
    f_r,
    b_s,
    b_r,
    lb_s,
    lb_r,
    lx_s,
    lx_r,
    lc_s,
    lc_r,
    hb_s,
    hb_r,
    hx_s,
    hx_r,
    hc_s,
    hc_r,
    t1_s,
    t1_r,
    t2_s,
    t2_r,
    z_s,
    z_r,
    q_s,
    q_r,
    a1_s,
    a1_r,
    a2_s,
    a2_r,
    a3_s,
    a3_r,
    a4_s,
    a4_r,
):
    r = lax.axis_index("row")
    c = lax.axis_index("col")
    k = r % 2
    chip = r // 2
    p = chip % PLANE
    y = p // SIDE
    x = p % SIDE
    zh = r // 32
    z = zh * COLS + c
    sib = (r + 1 - 2 * k, c)
    far = ((1 - zh) * 32 + p * 2 + k, c)

    def plane(i):
        return (zh * 32 + i * 2 + k, c)

    def in_band(i):
        return (r, i)

    def along_z(i):
        return ((i // COLS) * 32 + p * 2 + k, i % COLS)

    parts = 4
    part = SLOTS // parts
    near_load = pltpu.make_async_copy(near_hbm, near, load_sem.at[parts])
    near_load.start()
    loads = [
        pltpu.make_async_copy(
            vals_hbm.at[pl.ds(i * part, part)], vals.at[pl.ds(i * part, part)], load_sem.at[i]
        )
        for i in range(parts)
    ]
    for load in loads:
        load.start()

    barrier = pltpu.get_barrier_semaphore()
    pl.semaphore_signal(barrier, inc=1, device_id=sib, device_id_type=MESH)
    for d in range(1, PLANE):
        pl.semaphore_signal(
            barrier, inc=1, device_id=plane((p + d) % PLANE), device_id_type=MESH
        )
    for d in range(1, 2 * COLS):
        pl.semaphore_signal(
            barrier, inc=1, device_id=along_z((z + d) % (2 * COLS)), device_id_type=MESH
        )

    chain_c[0] = jnp.zeros((K, BLK), F32)
    chain_f[0] = jnp.zeros((K, BLK), F32)
    deg_c[0] = jnp.zeros((1, BLK), F32)
    deg_f[0] = jnp.zeros((1, BLK), F32)

    def each_later(body, first):
        @pl.when(zh == 0)
        def _():
            loop(1, PLANE + 1, lambda i: body(PLANE + (p + i) % PLANE))

        loop(first, PLANE, lambda i: body(zh * PLANE + i))

    def mirror_core(m, chain, t1, r1):
        kind = t1.dtype

        def to_core(at):
            t1[at] = chain[idx[LAST_COL + at * 2 + 1 - k]].astype(kind)
            remote(t1.at[at], r1.at[at], t1_s.at[m, at], t1_r.at[m, at], sib).start()

        each_later(to_core, p + k)

    def mirror_plane(m, chain, t1, r1, t2, r2):
        kind = t2.dtype

        def to_chip(at):
            to, half = at % PLANE, at // PLANE
            remote(t1.at[at], r1.at[at], t1_s.at[m, at], t1_r.at[m, at], sib).wait_recv()
            both = (chain[idx[LAST_COL + at * 2 + k]] + r1[at].astype(F32)).astype(kind)

            @pl.when(to == p)
            def _():
                r2[PLANE + p] = both

            @pl.when(to != p)
            def _():
                t2[at] = both
                remote(
                    t2.at[at],
                    r2.at[half * PLANE + p],
                    t2_s.at[m, at],
                    t2_r.at[m, half * PLANE + p],
                    plane(to),
                ).start()

        each_later(to_chip, p + 1)

    def mirror_cross(m, r2, t2, xs, xr):
        @pl.when(zh == 0)
        def _():
            def add(i, total):
                source = (p + i) % PLANE
                at = PLANE + source
                remote(t2.at[at], r2.at[at], t2_s.at[m, at], t2_r.at[m, at], plane(source)).wait_recv()
                return total + r2[at].astype(F32)

            xs[...] = lax.fori_loop(1, PLANE, add, r2[PLANE + p].astype(F32))
            remote(xs, xr, z_s.at[m], z_r.at[m], far).start()

    def mirror_sum(m, acc, t1, r1, t2, r2, xs, xr):
        def add(i, total):
            at = zh * PLANE + i
            remote(t2.at[at], r2.at[at], t2_s.at[m, at], t2_r.at[m, at], plane(i)).wait_recv()
            return total + r2[at].astype(F32)

        acc[...] += lax.fori_loop(0, p, add, jnp.zeros(acc.shape, F32))

        @pl.when(k == 1)
        def _():
            remote(
                t1.at[chip], r1.at[chip], t1_s.at[m, chip], t1_r.at[m, chip], sib
            ).wait_recv()
            acc[...] += r1[chip].astype(F32)

        @pl.when(zh == 1)
        def _():
            remote(xs, xr, z_s.at[m], z_r.at[m], far).wait_recv()
            acc[...] += xr[...]

    def mirror_done(m, t1, r1, t2, r2, xs, xr):
        def core_sent(i):
            at = CHIPS - 1 - i
            remote(t1.at[at], r1.at[at], t1_s.at[m, at], t1_r.at[m, at], sib).wait_send()

        loop(0, CHIPS - chip - k, core_sent)

        def chip_sent(i):
            at = CHIPS - 1 - i

            @pl.when(at % PLANE != p)
            def _():
                remote(
                    t2.at[at], r2.at[at], t2_s.at[m, at], t2_r.at[m, at], plane(at % PLANE)
                ).wait_send()

        loop(0, CHIPS - 1 - chip, chip_sent)

        @pl.when(zh == 0)
        def _():
            remote(xs, xr, z_s.at[m], z_r.at[m], far).wait_send()

    def band_send(m, wq, rq):
        for d in range(1, COLS):
            to = (c + d) % COLS
            remote(wq.at[to], rq.at[c], q_s.at[m, to], q_r.at[m, c], in_band(to)).start()

    def band_sum(m, acc, wq, rq):
        for d in range(1, COLS):
            at = (c + d) % COLS
            remote(wq.at[at], rq.at[at], q_s.at[m, at], q_r.at[m, at], in_band(at)).wait_recv()
            acc[...] += rq[at].astype(F32)

    def band_done(m, wq, rq):
        for d in range(1, COLS):
            at = (c + d) % COLS
            remote(wq.at[at], rq.at[at], q_s.at[m, at], q_r.at[m, at], in_band(at)).wait_send()

    cross = 32 + p * 2 + k
    place = (x, y)

    def line_of(half, i):
        return y * SIDE + i if half == 0 else i * SIDE + x

    def gather_copy(n, send, recv, at, device):
        block = gath.at[at]
        return remote(block, block, send, recv, device)

    def half_copy(n, half, send, recv, at, device):
        block = raw.at[n, at, pl.ds(half * HALF, HALF)]
        return remote(block, block, send, recv, device)

    def first_copy(n, half, i, source, device):
        at = line_of(half, source)
        return half_copy(n, half, c_s.at[n, half, i], c_r.at[n, half, source], at, plane(device))

    def second_copy(n, half, e, d):
        source = line_of(half, (place[half] + e) % SIDE)
        to = line_of(1 - half, (place[1 - half] + d) % SIDE)
        return half_copy(
            n, half, c2_s.at[n, half, e, d], c2_r.at[n, half, source], source, plane(to)
        )

    def band_copy(n, to, source, device):
        block = band_raw.at[n, source]
        return remote(block, block, b_s.at[n, to], b_r.at[n, source], in_band(device))

    def far_copy(n):
        return remote(band_raw.at[n, c], raw.at[n, p], x_s.at[n], x_r.at[n], far)

    def own_copy(n, to, source, at, device):
        return gather_copy(n, g_s.at[n, to], g_r.at[n, source], at, plane(device))

    def core_copy(n, at):
        return gather_copy(n, f_s.at[n, at], f_r.at[n, at], at, sib)

    def gather_far(n):
        @pl.when(zh == 1)
        def _():
            far_copy(n).start()

    def gather_band(n):
        for d in range(1, COLS):
            to = (c + d) % COLS
            band_copy(n, to, c, to).start()

    def gather_own(n):
        loop(1, p + 1, lambda i: own_copy(n, p - i, p, r, p - i).start())

        @pl.when(k == 1)
        def _():
            core_copy(n, r).start()

    def probe_of(line, block):
        return (line * nn(inverse[...], block, HIGH)).astype(BF16)

    def gather_first(n):
        @pl.when(zh == 0)
        def _():
            far_copy(n).wait_recv()
            for half in range(2):
                for d in range(1, SIDE):
                    to = (place[half] + d) % SIDE
                    first_copy(n, half, to, place[half], line_of(half, to)).start()
            for half in range(2):
                for d in range(1, SIDE):
                    second_copy(n, half, 0, d).start()

    def gather_second(n):
        @pl.when(zh == 0)
        def _():
            for e in range(1, SIDE):
                for half in range(2):
                    source = (place[half] + e) % SIDE
                    first_copy(n, half, source, source, line_of(half, source)).wait_recv()
                    for d in range(1, SIDE):
                        second_copy(n, half, e, d).start()

    def pass_own(n):
        def own_pass(i):
            at = zh * 32 + i * 2 + k
            own_copy(n, i, i, at, i).wait_recv()
            core_copy(n, at).start()

        loop(p + 1, PLANE, own_pass)

    def pass_cross(n):
        @pl.when(zh == 0)
        def _():
            def cross_pass(i):
                source = (p + i) % PLANE
                at = 32 + source * 2 + k
                for half, same in ((0, source // SIDE == y), (1, source % SIDE == x)):

                    @pl.when(jnp.logical_and(n > 0, jnp.logical_not(same)))
                    def _():
                        half_copy(
                            n,
                            half,
                            c2_s.at[n, half, 0, 0],
                            c2_r.at[n, half, source],
                            source,
                            plane(source),
                        ).wait_recv()

                gath[at] = probe_of(cross_lines[source], raw[n, source])
                core_copy(n, at).start()

            loop(0, PLANE, cross_pass)

    def gather_wait(n):
        loop(p + k, PLANE, lambda i: core_copy(n, zh * 32 + i * 2 + 1 - k).wait_recv())

        @pl.when(zh == 0)
        def _():
            loop(0, PLANE, lambda i: core_copy(n, 32 + i * 2 + 1 - k).wait_recv())

    def gather_z_done(n):
        for d in range(1, COLS):
            to = (c + d) % COLS
            band_copy(n, to, c, to).wait_send()

        @pl.when(zh == 1)
        def _():
            far_copy(n).wait_send()

        @pl.when(zh == 0)
        def _():
            for half in range(2):
                for d in range(1, SIDE):
                    to = (place[half] + d) % SIDE
                    first_copy(n, half, to, place[half], line_of(half, to)).wait_send()
                    for e in range(SIDE):
                        second_copy(n, half, e, d).wait_send()

    def gather_done(n):
        loop(0, p, lambda i: own_copy(n, i, p, r, i).wait_send())

        @pl.when(k == 1)
        def _():
            core_copy(n, r).wait_send()

        loop(p + 1, PLANE, lambda i: core_copy(n, zh * 32 + i * 2 + k).wait_send())

        @pl.when(zh == 0)
        def _():
            loop(0, PLANE, lambda i: core_copy(n, 32 + i * 2 + k).wait_send())

    code_high = codes[...].astype(BF16)
    code_rest = codes[...] - code_high.astype(F32)
    code_middle = code_rest.astype(BF16)
    code_low = (code_rest - code_middle.astype(F32)).astype(BF16)
    code_parts[...] = jnp.concatenate([code_high, code_middle, code_low], axis=0)

    def start_of(hole):
        onehot = jnp.where(
            lax.broadcasted_iota(jnp.int32, (codes.shape[1], BLK), 0) == hole, 1.0, 0.0
        ).astype(BF16)
        picked = nn(code_parts[...], onehot)
        return picked[:K] + picked[K : 2 * K] + picked[2 * K :]

    def hole_band_copy(to, source, device):
        return remote(
            holes, hole_band.at[source], hb_s.at[to], hb_r.at[source], in_band(device)
        )

    def hole_far_copy():
        return remote(holes, hole_cross.at[p], hx_s.at[0], hx_r.at[0], far)

    def hole_plane_copy(to, source, device):
        block = hole_cross.at[source]
        return remote(block, block, hc_s.at[to], hc_r.at[source], plane(device))

    band_raw[0, c] = start_of(holes[...])
    inverse[...] = jnp.where(
        lax.broadcasted_iota(jnp.int32, (K, K), 0) == lax.broadcasted_iota(jnp.int32, (K, K), 1),
        1.0,
        0.0,
    ).astype(F32)

    ones = jnp.ones((8, BLK), BF16)
    for i in range(parts):
        loads[i].wait()

        def sums(g):
            slots = [g * SUMS + u for u in range(SUMS)]
            down = [nn(ones, vals[s])[0:1] for s in slots]
            across = [nt(ones, vals[s])[0:1] for s in slots]
            for u, s in enumerate(slots):
                deg_c[s + 1] = deg_c[idx[PREV_COL + s]] + down[u]
                deg_f[s + 1] = deg_f[idx[PREV_ROW + s]] + across[u]

        loop(i * part // SUMS, (i + 1) * part // SUMS, sums)
    near_load.wait()
    pl.semaphore_wait(barrier, 1 + PLANE - 1 + 2 * COLS - 1)
    for d in range(1, COLS):
        to = (c + d) % COLS
        hole_band_copy(to, c, to).start()

    @pl.when(zh == 1)
    def _():
        hole_far_copy().start()


    mirror_core(0, deg_c, dt1, dr1)
    own_sum = jnp.zeros((1, BLK), F32)
    for q in range(COLS):
        tile = near[:, q * BLK : (q + 1) * BLK]
        own_sum = own_sum + nt(ones, tile)[0:1]
        dwq[q] = deg_f[idx[LAST_ROW + q]] + nn(ones, tile)[0:1]
    dacc[...] = own_sum + dwq[c]
    band_send(0, dwq, drq)
    mirror_plane(0, deg_c, dt1, dr1, dt2, dr2)

    @pl.when(zh == 0)
    def _():
        hole_far_copy().wait_recv()

        def hole_start(i):
            to = (p + i) % PLANE
            hole_plane_copy(to, p, to).start()

        loop(1, PLANE, hole_start)

    for d in range(1, COLS):
        at = (c + d) % COLS
        hole_band_copy(at, at, at).wait_recv()
        band_raw[0, at] = start_of(hole_band[at])
    mirror_cross(0, dr2, dt2, dxs, dxr)
    band_sum(0, dacc, dwq, drq)
    mirror_sum(0, dacc, dt1, dr1, dt2, dr2, dxs, dxr)
    scale = 1.0 / jnp.sqrt(dacc[...])

    def line_far():
        return remote(band_lines.at[c], cross_lines.at[p], lx_s.at[0], lx_r.at[0], far)

    def line_band(to, source, device):
        block = band_lines.at[source]
        return remote(block, block, lb_s.at[to], lb_r.at[source], in_band(device))

    band_lines[c] = scale
    for d in range(1, COLS):
        to = (c + d) % COLS
        line_band(to, c, to).start()

    @pl.when(zh == 1)
    def _():
        line_far().start()

    @pl.when(zh == 0)
    def _():
        raw[0, p] = start_of(hole_cross[p])

        def hole_wait(i):
            source = (p + i) % PLANE
            hole_plane_copy(source, source, source).wait_recv()
            raw[0, source] = start_of(hole_cross[source])

        loop(1, PLANE, hole_wait)

    mirror_done(0, dt1, dr1, dt2, dr2, dxs, dxr)
    band_done(0, dwq, drq)
    for d in range(1, COLS):
        at = (c + d) % COLS
        line_band(at, at, at).wait_recv()

    def line_plane(to, source, device):
        block = cross_lines.at[source]
        return remote(block, block, lc_s.at[to], lc_r.at[source], plane(device))

    @pl.when(zh == 0)
    def _():
        line_far().wait_recv()

        def to_plane(i):
            to = (p + i) % PLANE
            line_plane(to, p, to).start()

        loop(1, PLANE, to_plane)

    def lines_wait():
        @pl.when(zh == 0)
        def _():
            def arrived(i):
                source = (p + i) % PLANE
                line_plane(source, source, source).wait_recv()

            loop(1, PLANE, arrived)

    def lines_done():
        for d in range(1, COLS):
            to = (c + d) % COLS
            line_band(to, c, to).wait_send()
            hole_band_copy(to, c, to).wait_send()

        @pl.when(zh == 1)
        def _():
            line_far().wait_send()
            hole_far_copy().wait_send()

        @pl.when(zh == 0)
        def _():
            def line_sent(i):
                to = (p + i) % PLANE
                line_plane(to, p, to).wait_send()
                hole_plane_copy(to, p, to).wait_send()

            loop(1, PLANE, line_sent)

    def sweep(it):
        @pl.when(it > 0)
        def _():
            for d in range(1, COLS):
                at = (c + d) % COLS
                band_copy(it, at, at, at).wait_recv()

        for q in range(COLS):
            band[q] = probe_of(band_lines[q], band_raw[it, q])
        gath[r] = band[c]
        gather_own(it)

        def backward(g):
            slots = [g * GROUP + u for u in range(GROUP)]
            tiles = [nn(band[idx[ROW + s]], vals[s]) for s in slots]
            for s, tile in zip(slots, tiles):
                chain_c[s + 1] = chain_c[idx[PREV_COL + s]] + tile

        loop(0, SLOTS // GROUP, backward)
        mirror_core(1, chain_c, t1, r1)

        mirror_plane(1, chain_c, t1, r1, t2, r2)

        own = jnp.zeros((K, BLK), F32)
        for q in range(COLS):
            own = own + nt(band[q], near[:, q * BLK : (q + 1) * BLK])
        acc[...] = own


        pass_own(it)
        pl.when(it == 0)(lines_wait)
        pass_cross(it)
        gather_wait(it)

        mirror_cross(1, r2, t2, xs, xr)

        def forward(g):
            slots = [g * GROUP + u for u in range(GROUP)]
            tiles = [nt(gath[idx[COL + s]], vals[s]) for s in slots]
            for s, tile in zip(slots, tiles):
                chain_f[s + 1] = chain_f[idx[PREV_ROW + s]] + tile

        loop(0, SLOTS // GROUP, forward)
        probe = band[c]
        for q in range(COLS):
            total = chain_f[idx[LAST_ROW + q]] + nn(probe, near[:, q * BLK : (q + 1) * BLK])
            wq[q] = total.astype(BF16)

            @pl.when(c == q)
            def _():
                acc[...] += total

        band_send(1, wq, rq)
        gather_done(it)
        pl.when(it == 0)(lines_done)
        band_sum(1, acc, wq, rq)
        mirror_sum(1, acc, t1, r1, t2, r2, xs, xr)

        image = scale * acc[...]
        more = it < ITERS - 1

        @pl.when(more)
        def _():
            band_raw[it + 1, c] = image
            gather_far(it + 1)
            gather_band(it + 1)

        def when_more(stage):
            pl.when(more)(lambda: stage(it + 1))

        gram = nt(image, image, HIGH)

        low = jnp.concatenate([gram[0:16], gram[16:32]], axis=1)
        high = jnp.concatenate([gram[32:48], gram[48:64]], axis=1)
        gram_send[it] = jnp.where(k == 0, high, low)
        core = remote(gram_send.at[it], gram_core.at[it], a1_s.at[it], a1_r.at[it], sib)
        core.start()
        core.wait_recv()
        gram_plane[it, p] = jnp.where(k == 0, low, high) + gram_core[it]

        def plane_copy(to, source, device):
            block = gram_plane.at[it, source]
            return remote(block, block, a2_s.at[it, to], a2_r.at[it, source], plane(device))

        def plane_start(i):
            to = (p + i) % PLANE
            plane_copy(to, p, to).start()

        loop(1, PLANE, plane_start)

        def plane_wait(i):
            source = (p + i) % PLANE
            plane_copy(source, source, source).wait_recv()

        loop(1, PLANE, plane_wait)
        total = gram_plane[it, 0]
        for i in range(1, PLANE):
            total = total + gram_plane[it, i]
        gram_z[it, z] = total

        def z_copy(to, source, device):
            block = gram_z.at[it, source]
            return remote(block, block, a3_s.at[it, to], a3_r.at[it, source], along_z(device))

        for d in range(1, 2 * COLS):
            to = (z + d) % (2 * COLS)
            z_copy(to, z, to).start()
        when_more(gather_first)

        mirror_done(1, t1, r1, t2, r2, xs, xr)
        band_done(1, wq, rq)
        pl.when(it > 0)(lambda: gather_z_done(it))
        core.wait_send()

        def plane_done(i):
            to = (p + i) % PLANE
            plane_copy(to, p, to).wait_send()

        loop(1, PLANE, plane_done)
        for d in range(1, 2 * COLS):
            at = (z + d) % (2 * COLS)
            z_copy(at, at, at).wait_recv()
        total = gram_z[it, 0]
        for i in range(1, 2 * COLS):
            total = total + gram_z[it, i]
        gram_back[it, k] = total

        def back_copy(half):
            block = gram_back.at[it, half]
            return remote(block, block, a4_s.at[it], a4_r.at[it, half], sib)

        back_copy(k).start()
        when_more(gather_second)
        for d in range(1, 2 * COLS):
            to = (z + d) % (2 * COLS)
            z_copy(to, z, to).wait_send()
        back_copy(1 - k).wait_recv()
        low = gram_back[it, 0]
        high = gram_back[it, 1]
        gram = jnp.concatenate([low[:, :K], low[:, K:], high[:, :K], high[:, K:]], axis=0)
        total_rows = BLK * BANDS * COLS
        inverse[...] = inverse_factor(gram * (1.0 / total_rows))

        @pl.when(it == ITERS - 1)
        def _():
            out[...] = nn(inverse[...], image, HIGH)

        back_copy(k).wait_send()

    loop(0, ITERS, sweep)


def shards(block_rows, block_cols, block_values, near_values, hole_ids, start_codes):
    row_index = lax.axis_index("row")
    rows = block_rows.reshape(SLOTS)
    cols = block_cols.reshape(SLOTS)
    live = rows >= 0
    local_row = jnp.where(live, rows - row_index * COLS, -1)
    local_col = jnp.where(live, cols // COLS, -1)
    slot = jnp.arange(SLOTS, dtype=jnp.int32)

    def previous(keys):
        same = (keys[None, :] == keys[:, None]) & (slot[None, :] < slot[:, None])
        return jnp.max(jnp.where(same, slot[None, :] + 1, 0), axis=1)

    def last(keys):
        same = keys[None, :] == slot[:, None]
        return jnp.max(jnp.where(same, slot[None, :] + 1, 0), axis=1)

    idx = jnp.concatenate(
        [
            jnp.maximum(local_row, 0),
            jnp.maximum(local_col, 0),
            previous(local_col),
            previous(local_row),
            last(local_col),
            last(local_row),
        ]
    ).astype(jnp.int32)
    block = (K, BLK)
    line = (1, BLK)
    dma = pltpu.SemaphoreType.DMA
    return pl.pallas_call(
        kernel,
        name="subspace",
        out_shape=jax.ShapeDtypeStruct((K, BLK), F32),
        in_specs=[
            pl.BlockSpec(memory_space=pltpu.SMEM),
            pl.BlockSpec(memory_space=pl.ANY),
            pl.BlockSpec(memory_space=pl.ANY),
            pl.BlockSpec(memory_space=pltpu.VMEM),
            pl.BlockSpec(memory_space=pltpu.VMEM),
        ],
        out_specs=pl.BlockSpec(memory_space=pltpu.VMEM),
        scratch_shapes=[
            pltpu.VMEM((SLOTS, BLK, BLK), BF16),
            pltpu.VMEM((BLK, COLS * BLK), BF16),
            pltpu.VMEM((ITERS, PLANE, *block), F32),
            pltpu.VMEM((ITERS, COLS, *block), F32),
            pltpu.VMEM((PLANE, *line), F32),
            pltpu.VMEM((COLS, *line), F32),
            pltpu.VMEM((BANDS, *block), BF16),
            pltpu.VMEM((COLS, *block), BF16),
            pltpu.VMEM((SLOTS + 1, *block), F32),
            pltpu.VMEM((SLOTS + 1, *block), F32),
            pltpu.VMEM((SLOTS + 1, *line), F32),
            pltpu.VMEM((SLOTS + 1, *line), F32),
            pltpu.VMEM((CHIPS, *block), BF16),
            pltpu.VMEM((CHIPS, *block), BF16),
            pltpu.VMEM((CHIPS, *block), BF16),
            pltpu.VMEM((CHIPS, *block), BF16),
            pltpu.VMEM(block, F32),
            pltpu.VMEM(block, F32),
            pltpu.VMEM((COLS, *block), BF16),
            pltpu.VMEM((COLS, *block), BF16),
            pltpu.VMEM((CHIPS, *line), F32),
            pltpu.VMEM((CHIPS, *line), F32),
            pltpu.VMEM((CHIPS, *line), F32),
            pltpu.VMEM((CHIPS, *line), F32),
            pltpu.VMEM(line, F32),
            pltpu.VMEM(line, F32),
            pltpu.VMEM((3 * K, start_codes.shape[0]), BF16),
            pltpu.VMEM((COLS, *line), jnp.int32),
            pltpu.VMEM((PLANE, *line), jnp.int32),
            pltpu.VMEM((COLS, *line), F32),
            pltpu.VMEM((COLS, *line), F32),
            pltpu.VMEM(block, F32),
            pltpu.VMEM(line, F32),
            pltpu.VMEM((K, K), F32),
            pltpu.VMEM((ITERS, 16, 2 * K), F32),
            pltpu.VMEM((ITERS, 16, 2 * K), F32),
            pltpu.VMEM((ITERS, PLANE, 16, 2 * K), F32),
            pltpu.VMEM((ITERS, 2 * COLS, 16, 2 * K), F32),
            pltpu.VMEM((ITERS, 2, 16, 2 * K), F32),
            dma((5,)),
            dma((ITERS, PLANE)),
            dma((ITERS, PLANE)),
            dma((ITERS, 2, SIDE)),
            dma((ITERS, 2, SIDE)),
            dma((ITERS,)),
            dma((ITERS,)),
            dma((ITERS, 2, SIDE, SIDE)),
            dma((ITERS, 2, PLANE)),
            dma((ITERS, BANDS)),
            dma((ITERS, BANDS)),
            dma((ITERS, COLS)),
            dma((ITERS, COLS)),
            dma((COLS,)),
            dma((COLS,)),
            dma((1,)),
            dma((1,)),
            dma((PLANE,)),
            dma((PLANE,)),
            dma((COLS,)),
            dma((COLS,)),
            dma((1,)),
            dma((1,)),
            dma((PLANE,)),
            dma((PLANE,)),
            dma((2, CHIPS)),
            dma((2, CHIPS)),
            dma((2, CHIPS)),
            dma((2, CHIPS)),
            dma((2,)),
            dma((2,)),
            dma((2, COLS)),
            dma((2, COLS)),
            dma((ITERS,)),
            dma((ITERS,)),
            dma((ITERS, PLANE)),
            dma((ITERS, PLANE)),
            dma((ITERS, 2 * COLS)),
            dma((ITERS, 2 * COLS)),
            dma((ITERS,)),
            dma((ITERS, 2)),
        ],
        compiler_params=pltpu.CompilerParams(
            collective_id=0, has_side_effects=True, vmem_limit_bytes=56 << 20
        ),
    )(
        idx,
        block_values.reshape(SLOTS, BLK, BLK),
        near_values,
        hole_ids.reshape(1, BLK),
        start_codes.T,
    ).T


def solution(mesh):
    return jax.shard_map(
        shards,
        mesh=mesh,
        in_specs=(
            P("row", "col", None),
            P("row", "col", None),
            P("row", "col", None, None, None),
            P(("row", "col"), None),
            P(("row", "col")),
            P(),
        ),
        out_specs=P(("row", "col"), None),
        check_vma=False,
    )
```
